256 devices in a mesh: dp: 16 (over x, y_hi, core), ctx: 16 (over z, y_lo).
Axes of the slice: x: 4, y: 4 (y_hi: 2, y_lo: 2; y = y_hi * 2 + y_lo), z: 8, core: 2. Of those that a mesh axis runs over, the one named last changes fastest.
Arguments:
- queries: bfloat16 [16, 2048, 4096], P('dp', 'ctx'), may hold values from -5.5 to 5.5
- key_rows: bfloat16 [16, 2048, 512], P('dp', 'ctx'), may hold values from -5.5 to 5.5
- value_rows: bfloat16 [16, 2048, 512], P('dp', 'ctx'), may hold values from -6 to 6
- forward_out: bfloat16 [16, 2048, 4096], P('dp', 'ctx'), may hold values from -6 to 6
- out_grads: bfloat16 [16, 2048, 4096], P('dp', 'ctx'), may hold values from -6 to 6
- doc_lengths: int32 [16, 8], P('dp'), may hold values from 1 to 1024, 2048 in all within a row
- mask_tiers: int32 [16, 32, 32], P('dp'), may hold values from 0 to 2, as said below
- row_owners: int32 [16, 2048, 1], P('dp', 'ctx'), may hold values from 0 to 15; in each aligned block of 128 rows (0 to 127, 128 to 255, ..., all dimensions but the last counted through in order) at most 16 rows name the same one
Outputs:
- returned: bfloat16 [16, 16, 16, 16, 5120], P('dp', 'ctx')
The draws below stay inside these ranges and needn't reach their ends.
Inputs may be any that keep to these rules, and one draw needn't show every extreme that they name: `doc_lengths`: the 8 lengths of a pack sum to 2048. mask_tiers[p, b, b] is 1 or 2. `row_owners`: among the 128 positions of one device at most 16 name the same owner, and some device has an owner named exactly 16 times.
All inputs are finite; a program needn't handle non-finite values.
Results may differ from the reference program's by a relative error of at most 0.0048.
Values may be sent and summed in bfloat16 or wider, within the bound.
No kernel may reach another device: no remote copies, remote signals or barrier semaphores. Data moves between devices by JAX's collectives and lax.ppermute only.
A program may use at most 128 MiB of HBM per device.

```python
import math
import jax
import jax.numpy as jnp
import numpy as np
from jax import lax

H = 32
KV = 4
HD = 128
TOK_DEV = 128
MASK_BLK = 64
DOCS = 8
CAP = 16
SEQ = 2048
PACKS = 16
NB = 32
N_DP = 16
N_CTX = 16


def draw_queries(key, part):
    own_key = jax.random.fold_in(key, 7)
    shape = (PACKS, SEQ, H * HD)
    drawn = jnp.clip(jax.random.normal(own_key, shape, jnp.float32), -5.5, 5.5)
    return drawn.astype(jnp.bfloat16)


def draw_key_rows(key, part):
    own_key = jax.random.fold_in(key, 9)
    shape = (PACKS, SEQ, KV * HD)
    drawn = jnp.clip(jax.random.normal(own_key, shape, jnp.float32), -5.5, 5.5)
    return drawn.astype(jnp.bfloat16)


def draw_mask_tiers(key, part):
    key = jax.random.fold_in(key, 5)
    tiers = jax.random.randint(key, (PACKS, NB, NB), 0, 3, dtype=jnp.int32)
    diagonal = jax.random.randint(jax.random.fold_in(key, 1), (PACKS, NB, 1), 1, 3, dtype=jnp.int32)
    block_ids = jnp.arange(NB)
    on_diagonal = block_ids[:, None] == block_ids[None, :]
    return jnp.where(on_diagonal[None], diagonal, tiers)


def block_levels(stream_key, extent, cuts, smallest, largest):
    gain, own = 1.0, jax.random.fold_in(stream_key, 6)
    for axis_at, shards_of in cuts:
        heights = jnp.exp(jax.random.uniform(jax.random.fold_in(own, axis_at), (shards_of,), jnp.float32, smallest / len(cuts), largest / len(cuts)))
        gain = gain * jnp.repeat(heights, extent[axis_at] // shards_of).reshape([-1 if axis == axis_at else 1 for axis in range(len(extent))])
    return gain


def length_profile(number_of, total, reach, skew):
    loads = [(1 << 20) // math.isqrt(rank ** skew) + 1 for rank in range(2, number_of + 1)]
    spare, given = total - reach - (number_of - 1), [1] * (number_of - 1)
    while spare > 0:
        movable = [i for i in range(number_of - 1) if given[i] < reach]
        whole, budget = sum([loads[i] for i in movable]), spare
        for i in movable:
            extra = min(reach - given[i], max(1, budget * loads[i] // whole), spare)
            given[i] = given[i] + extra
            spare = spare - extra
    return np.array([reach] + given)


def uneven(key, number_of, total, limit, skew):
    if number_of == 2:
        one = jax.random.randint(key, (), max(1, total - limit), min(limit, total - 1) + 1)
        return jnp.stack([one, total - one])
    tallies = jnp.asarray(length_profile(number_of, total, limit, skew), jnp.int32)
    couples = (number_of - 1) // 2
    donor, receiver = tallies[1:1 + 2 * couples:2], tallies[2:2 + 2 * couples:2]
    slack = jnp.minimum(donor - 1, limit - receiver)
    shifted = jax.random.randint(jax.random.fold_in(key, 1), (couples,), 0, 1 << 20) % (slack + 1)
    tallies = tallies.at[1:1 + 2 * couples:2].set(donor - shifted).at[2:2 + 2 * couples:2].set(receiver + shifted)
    return tallies[jax.random.permutation(jax.random.fold_in(key, 2), number_of)]


def deal_out(key, own, number, rows, count, top, bound, slope):
    ranking = jax.random.permutation(key, count)
    packed, common = portions_of(count, rows * top, bound, slope, True), portions_of(count, rows * top, bound, slope, False)
    places = jnp.arange(count)

    def named(sizes, rotation):
        used = int((sizes > 0).sum())
        fixed = max(1, used // 4)
        passed = fixed + (places - fixed + rotation * (used - fixed)) % max(1, count - fixed)
        return jnp.zeros((count,), jnp.int32).at[ranking[jnp.where(places < fixed, places, passed)]].set(jnp.asarray(sizes, jnp.int32))

    sizes = jnp.where(number % 4 == 0, named(packed, number // 4), named(common, number - number // 4 - 1))
    mixed = jax.random.permutation(jax.random.fold_in(own, 3), count)
    source_of, sink = mixed[0:count // 2 * 2:2], mixed[1:count // 2 * 2:2]
    room = jnp.minimum(sizes[source_of] - 1, bound - sizes[sink]) // 2
    room = jnp.where((source_of == ranking[0]) | (sink == ranking[0]) | (sizes[sink] == 0), 0, jnp.maximum(room, 0))
    passed = jax.random.randint(jax.random.fold_in(own, 4), (count // 2,), 0, 1 << 20) % (room + 1)
    sizes = sizes.at[source_of].add(-passed).at[sink].add(passed)
    items = jnp.searchsorted(jnp.cumsum(sizes), jnp.arange(rows * top), side="right").astype(jnp.int32)
    listing = items.reshape(top, rows).T
    listing = listing[jax.random.permutation(jax.random.fold_in(own, 1), rows)]
    rotation = jax.random.randint(jax.random.fold_in(own, 2), (rows, 1), 0, top)
    return jnp.take_along_axis(listing, (jnp.arange(top)[None, :] + rotation) % top, axis=1)


def portions_of(amount, total, reach, skew, full):
    weights = [(1 << 20) // math.isqrt(rank ** skew) + 1 for rank in range(1, amount + 1)]
    largest = reach if full else min(reach, max(-(-total // amount), total * weights[0] // sum(weights)))
    least = 1 if total - largest >= amount - 1 else 0
    given, spare = [largest] + [least] * (amount - 1), total - largest - least * (amount - 1)
    while spare > 0:
        free = [i for i in range(1, amount) if given[i] < largest] or [i for i in range(1, amount) if given[i] < reach]
        whole, budget = sum([weights[i] for i in free]), spare
        for i in free:
            extra = min(reach - given[i], max(1, budget * weights[i] // whole), spare)
            given[i] = given[i] + extra
            spare = spare - extra
    return np.array(given)


def scatter_about(key, dims, width, reach, split=(), kind=jnp.bfloat16):
    level = block_levels(key, dims, split, -0.22, 0.18) if split else 1.0
    values = jax.random.normal(key, dims, jnp.float32) * width * level
    return jnp.minimum(jnp.maximum(values, -reach), reach).astype(kind)


def setup_inputs(seed: int = 0) -> dict:
    splits = jax.random.split(jax.random.key(seed), 9)
    queries = draw_queries(jax.random.fold_in(splits[8], 71), 0)
    key_rows = draw_key_rows(jax.random.fold_in(splits[8], 71), 0)
    value_rows = scatter_about(splits[2], (PACKS, SEQ, KV * HD), 1.0, 6.0, ((0, 16), (1, 16)))
    forward_out = scatter_about(splits[3], (PACKS, SEQ, H * HD), 1.0, 6.0, ((0, 16), (1, 16)))
    out_grads = scatter_about(splits[4], (PACKS, SEQ, H * HD), 1.0, 6.0, ((0, 16), (1, 16)))
    doc_lengths = jax.vmap(lambda own: uneven(own, DOCS, SEQ, SEQ // 2, 2))(jax.random.split(splits[5], PACKS)).reshape((PACKS, DOCS)).astype(jnp.int32)
    mask_tiers = draw_mask_tiers(jax.random.fold_in(splits[8], 71), 0)
    row_owners_keys = jax.random.split(jax.random.fold_in(splits[7], 1), PACKS * SEQ // TOK_DEV)
    row_owners_turns = jax.random.permutation(jax.random.fold_in(splits[7], 3), PACKS * SEQ // TOK_DEV)
    row_owners = jax.vmap(lambda own, number: deal_out(jax.random.fold_in(splits[7], 2), own, number, TOK_DEV, N_DP, 1, CAP, 2))(row_owners_keys, row_owners_turns).reshape((PACKS, SEQ, 1))
    return dict(queries=queries, key_rows=key_rows, value_rows=value_rows, forward_out=forward_out, out_grads=out_grads, doc_lengths=doc_lengths, mask_tiers=mask_tiers, row_owners=row_owners)


def doc_index(lengths, count):
    doc_ends = jnp.cumsum(lengths)
    places = jnp.arange(count, dtype=jnp.int32)
    return jnp.sum((places[:, None] >= doc_ends[None, :]).astype(jnp.int32), axis=1)


def pack_rows(operands):
    queries, key_rows, value_rows, forward_out, out_grads, lengths, tiers = operands
    groups = H // KV
    factor = HD ** -0.5
    query_heads = queries.reshape(SEQ, KV, groups, HD).astype(jnp.float32)
    grad_heads = out_grads.reshape(SEQ, KV, groups, HD).astype(jnp.float32)
    out_heads = forward_out.reshape(SEQ, KV, groups, HD).astype(jnp.float32)
    key_heads = key_rows.reshape(SEQ, KV, HD).astype(jnp.float32)
    value_heads = value_rows.reshape(SEQ, KV, HD).astype(jnp.float32)
    docs_all = doc_index(lengths, SEQ)
    places = jnp.arange(SEQ, dtype=jnp.int32)
    block_len = math.gcd(SEQ, 256)

    def query_block(running, block_index):
        key_grad, value_grad = running
        start = (block_index * block_len).astype(jnp.int32)
        query_part = lax.dynamic_slice_in_dim(query_heads, start, block_len, 0)
        grad_part = lax.dynamic_slice_in_dim(grad_heads, start, block_len, 0)
        out_part = lax.dynamic_slice_in_dim(out_heads, start, block_len, 0)
        query_pos = start + jnp.arange(block_len, dtype=jnp.int32)
        query_docs = lax.dynamic_slice_in_dim(docs_all, start, block_len, 0)
        tier_tile = tiers[query_pos // MASK_BLK][:, places // MASK_BLK]
        causal = places[None, :] <= query_pos[:, None]
        allowed = (query_docs[:, None] == docs_all[None, :]) & ((tier_tile == 2) | ((tier_tile == 1) & causal))
        scores = jnp.einsum("ikgd,jkd->kgij", query_part, key_heads) * factor
        row_max = jnp.max(jnp.where(allowed, scores, -1e30), axis=3)
        row_sum = jnp.sum(jnp.where(allowed, jnp.exp(scores - row_max[..., None]), 0.0), axis=3)
        lse = row_max + jnp.log(row_sum)
        weights = jnp.where(allowed, jnp.exp(scores - lse[..., None]), 0.0)
        weights_low = lax.optimization_barrier(weights.astype(jnp.bfloat16)).astype(jnp.float32)
        dprobs = jnp.einsum("ikgd,jkd->kgij", grad_part, value_heads)
        delta_rows = jnp.transpose(jnp.sum(grad_part * out_part, axis=3), (1, 2, 0))
        dscores = lax.optimization_barrier((weights * (dprobs - delta_rows[..., None])).astype(jnp.bfloat16)).astype(jnp.float32)
        dquery = (jnp.einsum("kgij,jkd->ikgd", dscores, key_heads) * factor).astype(jnp.bfloat16)
        key_grad = key_grad + jnp.einsum("kgij,ikgd->jkd", dscores, query_part)
        value_grad = value_grad + jnp.einsum("kgij,ikgd->jkd", weights_low, grad_part)
        return (key_grad, value_grad), dquery.reshape(block_len, H * HD)

    zero_grads = jnp.zeros((SEQ, KV, HD), jnp.float32)
    (key_grad, value_grad), dquery = lax.scan(query_block, (zero_grads, zero_grads), jnp.arange(SEQ // block_len, dtype=jnp.int32))
    dkey = (key_grad * factor).astype(jnp.bfloat16).reshape(SEQ, KV * HD)
    dvalue = value_grad.astype(jnp.bfloat16).reshape(SEQ, KV * HD)
    return jnp.concatenate([dquery.reshape(SEQ, H * HD), dkey, dvalue], axis=1)


def reference(queries, key_rows, value_rows, forward_out, out_grads, doc_lengths, mask_tiers, row_owners):
    rows_all = lax.map(pack_rows, (queries, key_rows, value_rows, forward_out, out_grads, doc_lengths, mask_tiers))
    owner_ids = row_owners[:, :, 0].reshape(N_DP, N_CTX, TOK_DEV)
    onehot = (owner_ids[..., None] == jnp.arange(N_DP, dtype=jnp.int32)).astype(jnp.int32)
    before = jnp.cumsum(onehot, axis=2) - onehot
    slot_ids = jnp.sum(before * onehot, axis=3)
    ctx_ids = jnp.broadcast_to(jnp.arange(N_CTX, dtype=jnp.int32)[None, :, None], owner_ids.shape)
    pack_ids = jnp.broadcast_to(jnp.arange(N_DP, dtype=jnp.int32)[:, None, None], owner_ids.shape)
    returned = jnp.zeros((N_DP, N_CTX, N_DP, CAP, H * HD + 2 * KV * HD), jnp.bfloat16)
    return returned.at[owner_ids, ctx_ids, pack_ids, slot_ids].set(rows_all.reshape(N_DP, N_CTX, TOK_DEV, H * HD + 2 * KV * HD))
```

```python
import math

import jax
import jax.numpy as jnp
from jax import lax
from jax.experimental import pallas as pl
from jax.experimental.pallas import tpu as pltpu
from jax.sharding import Mesh, PartitionSpec as P

H = 32
KV = 4
HD = 128
CAP = 16
N_DP = 16
NZ = 8
ROWS = 128
BLK = 2 * ROWS
HALF_Q = H * HD // 2
HALF_KV = KV * HD // 2
CHUNK = 2 * HD
STEPS = HALF_Q // CHUNK
SLOTS = N_DP * 2 * CAP
NEG = -1e30
F32 = jnp.float32
BF16 = jnp.bfloat16
NT = (((1,), (1,)), ((), ()))
NN = (((1,), (0,)), ((), ()))


def zshift(x, by):
    return lax.ppermute(x, "z", [(i, (i + by) % NZ) for i in range(NZ)])


def yswap(x):
    return lax.ppermute(x, "yl", [(0, 1), (1, 0)])


def grads_kernel(where_ref, ends_ref, tiers_ref, *refs):
    keys_in = refs[0:16]
    (q_own, q_par, g_own, g_par, delta_own, delta_par, t_own, t_par) = refs[16:24]
    packed_ref = refs[24]
    kv_out = refs[25:41]
    (kbuf, kt, sbuf, bias, acc, dqt, onehot, mx, active) = refs[41:]
    step = pl.program_id(0)
    z = where_ref[0]
    y = where_ref[1]
    factor = HD**-0.5
    to_log2 = factor * math.log2(math.e)

    @pl.when(step == 0)
    def _prepare():
        acc[...] = jnp.zeros_like(acc)
        target = jnp.concatenate([t_own[...], t_par[...]], axis=1)
        slot = lax.broadcasted_iota(jnp.int32, (SLOTS, BLK), 0)
        onehot[...] = jnp.where(slot == target, 1.0, 0.0).astype(BF16)
        lane = lax.broadcasted_iota(jnp.int32, (1, BLK), 1)
        query_pos = z * BLK + ((lane + ROWS * y) & (BLK - 1))
        first = jnp.zeros((1, BLK), jnp.int32)
        last = jnp.full((1, BLK), NZ * BLK, jnp.int32)
        for d in range(8):
            end = ends_ref[d]
            first = jnp.where(end <= query_pos, jnp.maximum(first, end), first)
            last = jnp.where(end > query_pos, jnp.minimum(last, end), last)
        last = last - 1
        low = jnp.int32(0)
        high = jnp.int32(NZ * BLK)
        for d in range(8):
            end = ends_ref[d]
            low = jnp.where(end <= z * BLK, jnp.maximum(low, end), low)
            high = jnp.where(end > z * BLK + BLK - 1, jnp.minimum(high, end), high)
        count = jnp.int32(0)
        for r in range(NZ):
            zb = (z - r) & (NZ - 1)
            kbuf[r, 0:ROWS, :] = keys_in[2 * r][...]
            kbuf[r, ROWS:BLK, :] = keys_in[2 * r + 1][...]
            needed = (zb * BLK < high) & (zb * BLK + BLK > low)
            active[count] = r
            count = count + needed.astype(jnp.int32)

            @pl.when(needed)
            def _block(r=r, zb=zb):
                for g in range(2):
                    kt[r, g] = kbuf[r, :, g * HD : (g + 1) * HD].T
                for jb in range(4):
                    j_base = zb * BLK + ROWS * (y ^ (jb // 2)) + 64 * (jb % 2)
                    j_blk = zb * 4 + 2 * (y ^ (jb // 2)) + jb % 2
                    key_pos = j_base + lax.broadcasted_iota(jnp.int32, (64, ROWS), 0)
                    for ip in range(2):
                        i_blk = z * 4 + 2 * (y ^ ip)
                        tier = jnp.where(
                            lax.broadcasted_iota(jnp.int32, (1, ROWS), 1) < 64,
                            tiers_ref[i_blk * 32 + j_blk],
                            tiers_ref[(i_blk + 1) * 32 + j_blk],
                        )
                        cols = slice(ip * ROWS, (ip + 1) * ROWS)
                        reach = jnp.where(tier == 2, NZ * BLK, jnp.where(tier == 1, query_pos[:, cols], -1))
                        upper = jnp.minimum(reach, last[:, cols])
                        ok = (key_pos >= first[:, cols]) & (key_pos <= upper)
                        bias[r, jb * 64 : (jb + 1) * 64, cols] = jnp.where(ok, 0.0, NEG)

        active[NZ] = count

    kv_head = step // (STEPS // 2)
    n_active = active[NZ]
    q = jnp.concatenate([q_own[:, :HD], q_par[:, :HD], q_own[:, HD:], q_par[:, HD:]], axis=0)
    g = jnp.concatenate([g_own[:, :HD], g_par[:, :HD], g_own[:, HD:], g_par[:, HD:]], axis=0)
    delta = jnp.concatenate(
        [
            delta_own[pl.ds(2 * step, 1), :],
            delta_par[pl.ds(2 * step, 1), :],
            delta_own[pl.ds(2 * step + 1, 1), :],
            delta_par[pl.ds(2 * step + 1, 1), :],
        ],
        axis=1,
    )
    k_cols = pl.ds(pl.multiple_of(kv_head * HD, HD), HD)
    v_cols = pl.ds(pl.multiple_of(HALF_KV + kv_head * HD, HD), HD)
    mx[...] = jnp.full_like(mx, NEG)
    dqt[...] = jnp.zeros_like(dqt)

    def score(n, carry):
        r = active[n]
        s = lax.dot_general(kbuf[r, :, k_cols], q, NT, preferred_element_type=F32)
        b = bias[r]
        s = s * to_log2 + jnp.concatenate([b, b], axis=1)
        sbuf[r] = s
        mx[...] = jnp.maximum(mx[...], jnp.max(s.reshape(BLK // 8, 8, 2 * BLK), axis=0))
        return carry

    lax.fori_loop(0, n_active, score, 0)
    top = jnp.max(mx[...], axis=0, keepdims=True)
    mx[...] = jnp.zeros_like(mx)

    def exponent(n, carry):
        r = active[n]
        p = jnp.exp2(sbuf[r] - top)
        sbuf[r] = p
        mx[...] += jnp.sum(p.reshape(BLK // 8, 8, 2 * BLK), axis=0)
        return carry

    lax.fori_loop(0, n_active, exponent, 0)
    inverse = 1.0 / jnp.sum(mx[...], axis=0, keepdims=True)

    def backward(n, carry):
        r = active[n]
        w = sbuf[r] * inverse
        dp = lax.dot_general(kbuf[r, :, v_cols], g, NT, preferred_element_type=F32)
        ds = (w * (dp - delta)).astype(BF16)
        acc[r, :, v_cols] += lax.dot_general(w.astype(BF16), g, NN, preferred_element_type=F32)
        acc[r, :, k_cols] += lax.dot_general(ds, q, NN, preferred_element_type=F32)
        dqt[...] += lax.dot_general(kt[r, kv_head], ds, NN, preferred_element_type=F32)
        return carry

    lax.fori_loop(0, n_active, backward, 0)
    low_dq = (dqt[...] * factor).astype(BF16)
    for h in range(2):
        packed_ref[:, h * HD : (h + 1) * HD] = lax.dot_general(
            onehot[...], low_dq[:, h * BLK : (h + 1) * BLK], NT, preferred_element_type=F32
        ).astype(BF16)

    @pl.when(step == STEPS - 1)
    def _finish():
        for r in range(NZ):
            for half in range(2):
                out = kv_out[2 * r + half]
                rows = slice(half * ROWS, (half + 1) * ROWS)
                out[:, :HALF_KV] = (acc[r, rows, :HALF_KV] * factor).astype(out.dtype)
                out[:, HALF_KV:] = acc[r, rows, HALF_KV:].astype(out.dtype)


def attention_grads(where, ends, tiers, keys, q_all, q_par, g_all, g_par, delta_own, delta_par, t_own, t_par):
    whole = pl.BlockSpec(memory_space=pltpu.VMEM)
    own = pl.BlockSpec((ROWS, CHUNK), lambda c, where, ends, tiers: (0, where[1] * STEPS + c))
    partner = pl.BlockSpec((ROWS, CHUNK), lambda c, where, ends, tiers: (0, c))
    block = jax.ShapeDtypeStruct((ROWS, 2 * HALF_KV), BF16)
    block_f32 = jax.ShapeDtypeStruct((ROWS, 2 * HALF_KV), F32)
    return pl.pallas_call(
        grads_kernel,
        grid_spec=pltpu.PrefetchScalarGridSpec(
            num_scalar_prefetch=3,
            grid=(STEPS,),
            in_specs=[whole] * 16 + [own, partner, own, partner] + [whole] * 4,
            out_specs=[pl.BlockSpec((SLOTS, CHUNK), lambda c, where, ends, tiers: (0, c))] + [whole] * 16,
            scratch_shapes=[
                pltpu.VMEM((NZ, BLK, 2 * HALF_KV), BF16),
                pltpu.VMEM((NZ, 2, HD, BLK), BF16),
                pltpu.VMEM((NZ, BLK, 2 * BLK), F32),
                pltpu.VMEM((NZ, BLK, BLK), F32),
                pltpu.VMEM((NZ, BLK, 2 * HALF_KV), F32),
                pltpu.VMEM((HD, 2 * BLK), F32),
                pltpu.VMEM((SLOTS, BLK), BF16),
                pltpu.VMEM((8, 2 * BLK), F32),
                pltpu.SMEM((NZ + 1,), jnp.int32),
            ],
        ),
        out_shape=[jax.ShapeDtypeStruct((SLOTS, HALF_Q), BF16)] + [block_f32] * 2 + [block] * 14,
        compiler_params=pltpu.CompilerParams(
            dimension_semantics=("arbitrary",), vmem_limit_bytes=48 * 1024 * 1024
        ),
        cost_estimate=pl.CostEstimate(flops=8 * 10**9, bytes_accessed=10 * 2**20, transcendentals=4 * 10**6),
        name="grads",
    )(where, ends, tiers, *keys, q_all, q_par, g_all, g_par, delta_own, delta_par, t_own, t_par)


def finish_kernel(own_a, own_b, down_a, up_a, down_b, up_b, t_own, t_par, out):
    target = jnp.concatenate([t_own[...], t_par[...]], axis=1)
    slot = lax.broadcasted_iota(jnp.int32, (SLOTS, BLK), 0)
    onehot = jnp.where(slot == target, 1.0, 0.0).astype(BF16)
    a = own_a[...] + down_a[...].astype(F32) + up_a[...].astype(F32)
    b = own_b[...] + down_b[...].astype(F32) + up_b[...].astype(F32)
    rows = jnp.concatenate([a, b], axis=0).astype(BF16)
    out[...] = lax.dot_general(onehot, rows, NN, preferred_element_type=F32).astype(BF16)


def finish_rows(*operands):
    whole = pl.BlockSpec(memory_space=pltpu.VMEM)
    return pl.pallas_call(
        finish_kernel,
        in_specs=[whole] * 8,
        out_specs=whole,
        out_shape=jax.ShapeDtypeStruct((SLOTS, 2 * HALF_KV), BF16),
        compiler_params=pltpu.CompilerParams(vmem_limit_bytes=16 * 1024 * 1024),
        name="finish",
    )(*operands)


def lay_out_kernel(q_ref, kv_ref, out):
    for y in range(2):
        out[0, :, y * HALF_Q : (y + 1) * HALF_Q] = q_ref[y]
        for part in range(2):
            start = 2 * HALF_Q + part * 2 * HALF_KV + y * HALF_KV
            out[0, :, start : start + HALF_KV] = kv_ref[y, :, part * HALF_KV : (part + 1) * HALF_KV]


def lay_out(q_rows, kv_rows):
    width = 2 * HALF_Q + 4 * HALF_KV
    return pl.pallas_call(
        lay_out_kernel,
        grid=(N_DP,),
        in_specs=[
            pl.BlockSpec((2, CAP, HALF_Q), lambda n: (n, 0, 0)),
            pl.BlockSpec((2, CAP, 2 * HALF_KV), lambda n: (n, 0, 0)),
        ],
        out_specs=pl.BlockSpec((1, CAP, width), lambda n: (n, 0, 0)),
        out_shape=jax.ShapeDtypeStruct((N_DP, CAP, width), BF16),
        name="lay_out",
    )(q_rows, kv_rows)


def add_low(a, b):
    return (a.astype(F32) + b.astype(F32)).astype(BF16)


def per_device(queries, key_rows, value_rows, forward_out, out_grads, doc_lengths, mask_tiers, row_owners):
    z = lax.axis_index("z").astype(jnp.int32)
    y = lax.axis_index("yl").astype(jnp.int32)
    q_all, g_all = queries[0], out_grads[0]

    def half(x, which, width):
        return lax.dynamic_slice_in_dim(x, which * width, width, 1)

    def key_values(which):
        return jnp.concatenate(
            [half(key_rows[0], which, HALF_KV), half(value_rows[0], which, HALF_KV)], axis=1
        )

    a = key_values(y)
    b = yswap(key_values(1 - y))
    q_par = yswap(half(q_all, 1 - y, HALF_Q))
    g_par = yswap(half(g_all, 1 - y, HALF_Q))
    keys_a = {0: a}
    keys_b = {0: b}
    for hop in range(1, 4):
        for held in (keys_a, keys_b):
            held[hop] = zshift(held[hop - 1], 1)
            held[NZ - hop] = zshift(held[(NZ - hop + 1) % NZ], -1)
    keys_a[4] = zshift(keys_a[3], 1)
    keys_b[4] = zshift(keys_b[5], -1)

    owners = row_owners[0, :, 0]
    places = jnp.arange(ROWS, dtype=jnp.int32)
    earlier = (places[:, None] < places[None, :]) & (owners[:, None] == owners[None, :])
    slots = jnp.sum(earlier.astype(jnp.int32), axis=0)
    t_own = (owners * (2 * CAP) + y * CAP + slots)[None, :]
    t_par = yswap(t_own)
    delta = jnp.sum(
        g_all.reshape(ROWS, H, HD).astype(F32) * forward_out[0].reshape(ROWS, H, HD).astype(F32), axis=2
    ).T
    delta_own = lax.dynamic_slice_in_dim(delta, y * (H // 2), H // 2, 0)
    delta_par = yswap(lax.dynamic_slice_in_dim(delta, (1 - y) * (H // 2), H // 2, 0))
    ends = jnp.cumsum(doc_lengths[0])

    keys = []
    for r in range(NZ):
        keys += [keys_a[r], keys_b[r]]
    packed, own_a, own_b, *parts = attention_grads(
        jnp.stack([z, y]),
        ends,
        mask_tiers[0].reshape(-1),
        keys,
        q_all,
        q_par,
        g_all,
        g_par,
        delta_own,
        delta_par,
        t_own,
        t_par,
    )
    part_a = {r: parts[2 * (r - 1)] for r in range(1, NZ)}
    part_b = {r: parts[2 * (r - 1) + 1] for r in range(1, NZ)}

    down_a = zshift(part_a[4], -1)
    up_b = zshift(part_b[4], 1)
    for r in (3, 2, 1):
        down_a = zshift(add_low(down_a, part_a[r]), -1)
        up_b = zshift(add_low(up_b, part_b[NZ - r]), 1)
    down_b = zshift(part_b[3], -1)
    up_a = zshift(part_a[5], 1)
    for r in (2, 1):
        down_b = zshift(add_low(down_b, part_b[r]), -1)
        up_a = zshift(add_low(up_a, part_a[NZ - r]), 1)

    def to_owners(rows):
        width = rows.shape[1]
        return lax.all_to_all(
            rows.reshape(2 * N_DP, CAP, width), ("dp", "yl"), split_axis=0, concat_axis=0, tiled=True
        )

    q_rows = to_owners(packed)
    kv_rows = to_owners(finish_rows(own_a, own_b, down_a, up_a, down_b, up_b, t_own, t_par))
    return lay_out(q_rows, kv_rows)[None, None]


def solution(mesh):
    fine = Mesh(mesh.devices.reshape(N_DP, NZ, 2), ("dp", "z", "yl"))
    rows = P("dp", ("z", "yl"), None)
    return jax.shard_map(
        per_device,
        mesh=fine,
        in_specs=(rows, rows, rows, rows, rows, P("dp", None), P("dp", None, None), rows),
        out_specs=P("dp", ("z", "yl"), None, None, None),
        check_vma=False,
    )
```

```python
import math

import jax
import jax.numpy as jnp
from jax import lax
from jax.experimental import pallas as pl
from jax.experimental.pallas import tpu as pltpu
from jax.sharding import Mesh, PartitionSpec as P

H = 32
KV = 4
HD = 128
CAP = 16
N_DP = 16
NZ = 8
ROWS = 128
BLK = 2 * ROWS
HALF_Q = H * HD // 2
HALF_KV = KV * HD // 2
HEADS_KV = H // KV
STEP_HEADS = 8
CHUNK = STEP_HEADS * HD
WIDTH = STEP_HEADS * ROWS
STEPS = 2 * HALF_Q // CHUNK
SLOTS = N_DP * 2 * CAP
LAY_OUT = 4
NEG = -1e30
F32 = jnp.float32
BF16 = jnp.bfloat16
NT = (((1,), (1,)), ((), ()))
NN = (((1,), (0,)), ((), ()))


def zshift(x, by):
    return lax.ppermute(x, "z", [(i, (i + by) % NZ) for i in range(NZ)])


def yswap(x):
    return lax.ppermute(x, "yl", [(0, 1), (1, 0)])


def zshift_yswap(x, by):
    pairs = [(2 * i + y, 2 * ((i + by) % NZ) + 1 - y) for i in range(NZ) for y in range(2)]
    return lax.ppermute(x, ("z", "yl"), pairs)


def slots_of(extra, pair_place):
    owner = extra[3 * H // 2 : 3 * H // 2 + 1].astype(jnp.int32)
    return owner * (2 * CAP) + pair_place * CAP + extra[3 * H // 2 + 1 : 3 * H // 2 + 2].astype(jnp.int32)


def grads_kernel(where_ref, ends_ref, tiers_ref, *refs):
    keys_in = refs[0:16]
    q_own, q_par, g_own, g_par, extra_own, extra_par, packed_ref = refs[16:23]
    kv_out = refs[23:39]
    (kbuf, kt, sbuf, bias, acc, dqt, onehot, mx, den, deltas, active) = refs[39:]
    step = pl.program_id(0)
    half = step // (STEPS // 2)
    z = where_ref[0]
    y = where_ref[1]
    factor = HD**-0.5
    to_log2 = factor * math.log2(math.e)

    @pl.when(step == 0)
    def _prepare():
        acc[...] = jnp.zeros_like(acc)
        for r in range(NZ):
            kbuf[r, 0:ROWS, :] = keys_in[2 * r][...]
            kbuf[r, ROWS:BLK, :] = keys_in[2 * r + 1][...]
            for g in range(2):
                kt[r, g] = kbuf[r, :, g * HD : (g + 1) * HD].T

    @pl.when(step % (STEPS // 2) == 0)
    def _mask():
        extra = jnp.where(half == 0, extra_own[...], extra_par[...]).astype(F32).T
        deltas[...] = extra[0 : H // 2] + extra[H // 2 : H] + extra[H : 3 * H // 2]
        target = slots_of(extra, y ^ half)
        base = z * BLK + ROWS * (y ^ half)
        slot = lax.broadcasted_iota(jnp.int32, (SLOTS // 2, ROWS), 0)
        slot = (slot // CAP) * (2 * CAP) + (y ^ half) * CAP + slot % CAP
        onehot[...] = jnp.where(slot == target, 1.0, 0.0).astype(BF16)
        query_pos = base + lax.broadcasted_iota(jnp.int32, (1, ROWS), 1)
        first = jnp.zeros((1, ROWS), jnp.int32)
        last = jnp.full((1, ROWS), NZ * BLK, jnp.int32)
        low = jnp.int32(0)
        high = jnp.int32(NZ * BLK)
        for d in range(8):
            end = ends_ref[d]
            first = jnp.where(end <= query_pos, jnp.maximum(first, end), first)
            last = jnp.where(end > query_pos, jnp.minimum(last, end), last)
            low = jnp.where(end <= base, jnp.maximum(low, end), low)
            high = jnp.where(end > base + ROWS - 1, jnp.minimum(high, end), high)
        last = last - 1
        i_blk = 4 * z + 2 * (y ^ half)
        count = jnp.int32(0)
        for r in range(NZ):
            zb = (z - r) & (NZ - 1)
            needed = (zb * BLK < high) & (zb * BLK + BLK > low)
            active[count] = r
            count = count + needed.astype(jnp.int32)

            @pl.when(needed)
            def _block(r=r, zb=zb):
                for jb in range(4):
                    j_blk = zb * 4 + 2 * (y ^ (jb // 2)) + jb % 2
                    key_pos = j_blk * 64 + lax.broadcasted_iota(jnp.int32, (64, ROWS), 0)
                    tier = jnp.where(
                        lax.broadcasted_iota(jnp.int32, (1, ROWS), 1) < 64,
                        tiers_ref[i_blk * 32 + j_blk],
                        tiers_ref[(i_blk + 1) * 32 + j_blk],
                    )
                    reach = jnp.where(tier == 2, NZ * BLK, jnp.where(tier == 1, query_pos, -1))
                    ok = (key_pos >= first) & (key_pos <= jnp.minimum(reach, last))
                    bias[r, jb * 64 : (jb + 1) * 64, :] = jnp.where(ok, 0.0, NEG)

        active[NZ] = count

    kv_head = (step // (HEADS_KV // STEP_HEADS)) % 2
    n_active = active[NZ]
    own = half == 0
    q_all = jnp.where(own, q_own[...], q_par[...])
    g_all = jnp.where(own, g_own[...], g_par[...])
    q = jnp.concatenate([q_all[:, h * HD : (h + 1) * HD] for h in range(STEP_HEADS)], axis=0)
    g = jnp.concatenate([g_all[:, h * HD : (h + 1) * HD] for h in range(STEP_HEADS)], axis=0)
    head = (step % (STEPS // 2)) * STEP_HEADS
    delta = jnp.concatenate([deltas[pl.ds(head + h, 1), :] for h in range(STEP_HEADS)], axis=1)
    k_cols = pl.ds(pl.multiple_of(kv_head * HD, HD), HD)
    v_cols = pl.ds(pl.multiple_of(HALF_KV + kv_head * HD, HD), HD)
    mx[...] = jnp.full_like(mx, NEG)
    den[...] = jnp.zeros_like(den)
    dqt[...] = jnp.zeros_like(dqt)

    def score(n, carry):
        r = active[n]
        s = lax.dot_general(kbuf[r, :, k_cols], q, NT, preferred_element_type=F32)
        b = bias[r]
        s = s * to_log2 + jnp.concatenate([b] * STEP_HEADS, axis=1)
        sbuf[r] = s
        s = s.reshape(BLK // 8, 8, WIDTH)
        old = mx[...]
        new = jnp.maximum(old, jnp.max(s, axis=0))
        mx[...] = new
        den[...] = den[...] * jnp.exp2(old - new) + jnp.sum(jnp.exp2(s - new[None]), axis=0)
        return carry

    def score_pair(n, carry):
        score(2 * n, 0)
        score(2 * n + 1, 0)
        return carry

    lax.fori_loop(0, n_active // 2, score_pair, 0)

    @pl.when(n_active % 2 == 1)
    def _score_last():
        score(n_active - 1, 0)

    top = jnp.max(mx[...], axis=0, keepdims=True)
    lse = top + jnp.log2(jnp.sum(den[...] * jnp.exp2(mx[...] - top), axis=0, keepdims=True))

    def backward(n, carry):
        r = active[n]
        w = jnp.exp2(sbuf[r] - lse)
        dp = lax.dot_general(kbuf[r, :, v_cols], g, NT, preferred_element_type=F32)
        ds = (w * (dp - delta)).astype(BF16)
        acc[r, :, v_cols] += lax.dot_general(w.astype(BF16), g, NN, preferred_element_type=F32)
        acc[r, :, k_cols] += lax.dot_general(ds, q, NN, preferred_element_type=F32)
        dqt[...] += lax.dot_general(kt[r, kv_head], ds, NN, preferred_element_type=F32)
        return carry

    def backward_pair(n, carry):
        backward(2 * n, 0)
        backward(2 * n + 1, 0)
        return carry

    lax.fori_loop(0, n_active // 2, backward_pair, 0)

    @pl.when(n_active % 2 == 1)
    def _backward_last():
        backward(n_active - 1, 0)

    low_dq = (dqt[...] * factor).astype(BF16)
    for h in range(STEP_HEADS):
        packed_ref[:, 0, :, h * HD : (h + 1) * HD] = (
            lax.dot_general(onehot[...], low_dq[:, h * ROWS : (h + 1) * ROWS], NT, preferred_element_type=F32)
            .astype(BF16)
            .reshape(N_DP, CAP, HD)
        )

    @pl.when(step == STEPS - 1)
    def _finish():
        for r in range(NZ):
            for part in range(2):
                out = kv_out[2 * r + part]
                rows = slice(part * ROWS, (part + 1) * ROWS)
                out[:, :HALF_KV] = (acc[r, rows, :HALF_KV] * factor).astype(out.dtype)
                out[:, HALF_KV:] = acc[r, rows, HALF_KV:].astype(out.dtype)


def attention_grads(where, ends, tiers, keys, q_all, qg_par, g_all, extra_own):
    block = pl.BlockSpec((ROWS, 2 * HALF_KV), lambda c, where, ends, tiers: (0, 0))
    extra = pl.BlockSpec((ROWS, HD), lambda c, where, ends, tiers: (0, 0))
    extra_par = pl.BlockSpec((ROWS, HD), lambda c, where, ends, tiers: (0, 2 * HALF_Q // HD))
    per_half = STEPS // 2

    def own_at(c, where, ends, tiers):
        return 0, where[1] * per_half + jnp.minimum(c, per_half - 1)

    def partner_at(c, where, ends, tiers):
        return 0, jnp.maximum(c - per_half, 0)

    def partner_g_at(c, where, ends, tiers):
        return 0, per_half + jnp.maximum(c - per_half, 0)

    def out_at(c, where, ends, tiers):
        return 0, where[1] ^ (c // per_half), 0, c % per_half

    own = pl.BlockSpec((ROWS, CHUNK), own_at)
    partner = pl.BlockSpec((ROWS, CHUNK), partner_at)
    partner_g = pl.BlockSpec((ROWS, CHUNK), partner_g_at)
    kv_bf16 = jax.ShapeDtypeStruct((ROWS, 2 * HALF_KV), BF16)
    kv_f32 = jax.ShapeDtypeStruct((ROWS, 2 * HALF_KV), F32)
    return pl.pallas_call(
        grads_kernel,
        grid_spec=pltpu.PrefetchScalarGridSpec(
            num_scalar_prefetch=3,
            grid=(STEPS,),
            in_specs=[block] * 16 + [own, partner, own, partner_g, extra, extra_par],
            out_specs=[pl.BlockSpec((N_DP, 1, CAP, CHUNK), out_at)] + [block] * 16,
            scratch_shapes=[
                pltpu.VMEM((NZ, BLK, 2 * HALF_KV), BF16),
                pltpu.VMEM((NZ, 2, HD, BLK), BF16),
                pltpu.VMEM((NZ, BLK, WIDTH), F32),
                pltpu.VMEM((NZ, BLK, ROWS), F32),
                pltpu.VMEM((NZ, BLK, 2 * HALF_KV), F32),
                pltpu.VMEM((HD, WIDTH), F32),
                pltpu.VMEM((SLOTS // 2, ROWS), BF16),
                pltpu.VMEM((8, WIDTH), F32),
                pltpu.VMEM((8, WIDTH), F32),
                pltpu.VMEM((H // 2, ROWS), F32),
                pltpu.SMEM((NZ + 1,), jnp.int32),
            ],
        ),
        out_shape=[jax.ShapeDtypeStruct((N_DP, 2, CAP, HALF_Q), BF16)] + [kv_f32] * 2 + [kv_bf16] * 14,
        compiler_params=pltpu.CompilerParams(
            dimension_semantics=("arbitrary",), vmem_limit_bytes=56 * 1024 * 1024
        ),
        cost_estimate=pl.CostEstimate(flops=8 * 10**9, bytes_accessed=10 * 2**20, transcendentals=4 * 10**6),
        name="grads",
    )(where, ends, tiers, *keys, q_all, qg_par, g_all, qg_par, extra_own, qg_par)


def finish_kernel(where_ref, own_a, own_b, down_a, up_a, down_b, up_b, extra_own, extra_par, out):
    y = where_ref[1]
    target = jnp.concatenate(
        [slots_of(extra_own[...].astype(F32).T, y), slots_of(extra_par[...].astype(F32).T, 1 - y)], axis=1
    )
    slot = lax.broadcasted_iota(jnp.int32, (SLOTS, BLK), 0)
    onehot = jnp.where(slot == target, 1.0, 0.0).astype(BF16)
    a = own_a[...] + down_a[...].astype(F32) + up_a[...].astype(F32)
    b = own_b[...] + down_b[...].astype(F32) + up_b[...].astype(F32)
    rows = jnp.concatenate([a, b], axis=0).astype(BF16)
    out[...] = lax.dot_general(onehot, rows, NN, preferred_element_type=F32).astype(BF16)


def finish_rows(*operands):
    block = pl.BlockSpec((ROWS, 2 * HALF_KV), lambda c, where: (0, 0))
    extra = pl.BlockSpec((ROWS, HD), lambda c, where: (0, 0))
    extra_par = pl.BlockSpec((ROWS, HD), lambda c, where: (0, 2 * HALF_Q // HD))
    return pl.pallas_call(
        finish_kernel,
        grid_spec=pltpu.PrefetchScalarGridSpec(
            num_scalar_prefetch=1,
            grid=(1,),
            in_specs=[block] * 6 + [extra, extra_par],
            out_specs=pl.BlockSpec((SLOTS, 2 * HALF_KV), lambda c, where: (0, 0)),
        ),
        out_shape=jax.ShapeDtypeStruct((SLOTS, 2 * HALF_KV), BF16),
        compiler_params=pltpu.CompilerParams(vmem_limit_bytes=16 * 1024 * 1024),
        name="finish",
    )(*operands)


def lay_out_kernel(q_ref, kv_ref, out):
    first = pl.program_id(0) * LAY_OUT
    for n in range(LAY_OUT):
        for y in range(2):
            out[n, :, y * HALF_Q : (y + 1) * HALF_Q] = q_ref[2 * (first + n) + y]
            for part in range(2):
                start = 2 * HALF_Q + part * 2 * HALF_KV + y * HALF_KV
                out[n, :, start : start + HALF_KV] = kv_ref[2 * (first + n) + y, :, part * HALF_KV : (part + 1) * HALF_KV]


def lay_out(q_rows, kv_rows):
    width = 2 * HALF_Q + 4 * HALF_KV
    whole = pl.BlockSpec(memory_space=pltpu.VMEM)
    return pl.pallas_call(
        lay_out_kernel,
        grid=(N_DP // LAY_OUT,),
        in_specs=[whole, whole],
        out_specs=pl.BlockSpec((LAY_OUT, CAP, width), lambda n: (n, 0, 0)),
        out_shape=jax.ShapeDtypeStruct((N_DP, CAP, width), BF16),
        compiler_params=pltpu.CompilerParams(vmem_limit_bytes=16 * 1024 * 1024),
        name="lay_out",
    )(q_rows, kv_rows)


def add_low(a, b):
    return (a.astype(F32) + b.astype(F32)).astype(BF16)


def prepare_kernel(where_ref, q_half, g_all, out_all, owners_ref, send, extra_own):
    y = where_ref[0]
    lane = lax.broadcasted_iota(jnp.int32, (ROWS, HD), 1)
    row = lax.broadcasted_iota(jnp.int32, (ROWS, HD), 0)
    owners = jnp.broadcast_to(owners_ref[...].astype(F32), (ROWS, HD))
    earlier = (owners == owners.T) & (lane < row)
    slots = jnp.sum(jnp.where(earlier, 1.0, 0.0), axis=1, keepdims=True)
    head = lax.broadcasted_iota(jnp.int32, (HALF_Q, HD), 0) // HD
    pick = jnp.where(head == lax.broadcasted_iota(jnp.int32, (HALF_Q, HD), 1), 1.0, 0.0).astype(BF16)

    def extras(which):
        cols = pl.ds(pl.multiple_of(which * HALF_Q, HALF_Q), HALF_Q)
        product = g_all[:, cols].astype(F32) * out_all[:, cols].astype(F32)
        upper = product.astype(BF16)
        lower = (product - upper.astype(F32)).astype(BF16)
        delta = lax.dot_general(upper, pick, NN, preferred_element_type=F32)
        delta += lax.dot_general(lower, pick, NN, preferred_element_type=F32)
        high = delta.astype(BF16).astype(F32)
        middle = (delta - high).astype(BF16).astype(F32)
        low = delta - high - middle
        terms = high + pltpu.roll(middle, H // 2, 1) + pltpu.roll(low, H, 1)
        terms = jnp.where(lane == 3 * H // 2, owners, jnp.where(lane == 3 * H // 2 + 1, slots, terms))
        return terms.astype(BF16)

    send[:, :HALF_Q] = q_half[...]
    send[:, HALF_Q : 2 * HALF_Q] = g_all[:, pl.ds(pl.multiple_of((1 - y) * HALF_Q, HALF_Q), HALF_Q)]
    send[:, 2 * HALF_Q :] = extras(1 - y)
    extra_own[...] = extras(y)


def prepare(y, q_all, g_all, out_all, owners):
    width = 2 * HALF_Q + HD

    def whole(shape):
        return pl.BlockSpec(shape, lambda n, where: (0, 0))

    return pl.pallas_call(
        prepare_kernel,
        grid_spec=pltpu.PrefetchScalarGridSpec(
            num_scalar_prefetch=1,
            grid=(1,),
            in_specs=[
                pl.BlockSpec((ROWS, HALF_Q), lambda n, where: (0, 1 - where[0])),
                whole((ROWS, 2 * HALF_Q)),
                whole((ROWS, 2 * HALF_Q)),
                whole((ROWS, 1)),
            ],
            out_specs=[whole((ROWS, width)), whole((ROWS, HD))],
        ),
        out_shape=[jax.ShapeDtypeStruct((ROWS, width), BF16), jax.ShapeDtypeStruct((ROWS, HD), BF16)],
        compiler_params=pltpu.CompilerParams(vmem_limit_bytes=56 * 1024 * 1024),
        name="prepare",
    )(y[None], q_all, g_all, out_all, owners)


def per_device(queries, key_rows, value_rows, forward_out, out_grads, doc_lengths, mask_tiers, row_owners):
    z = lax.axis_index("z").astype(jnp.int32)
    y = lax.axis_index("yl").astype(jnp.int32)
    q_all, g_all = queries[0], out_grads[0]

    def half(x, which, width):
        return lax.dynamic_slice_in_dim(x, which * width, width, 1)

    def key_values(which):
        return jnp.concatenate(
            [half(key_rows[0], which, HALF_KV), half(value_rows[0], which, HALF_KV)], axis=1
        )

    a = key_values(y)
    b = key_values(1 - y)
    keys_a = {0: a, 1: zshift(a, 1), 7: zshift(a, -1)}
    keys_b = {0: yswap(b), 1: zshift_yswap(b, 1), 7: zshift_yswap(b, -1)}
    send, extra_own = prepare(y, q_all, g_all, forward_out[0], row_owners[0])
    send, keys_b[0] = lax.optimization_barrier((send, keys_b[0]))
    qg_par = yswap(send)
    for hop in range(2, 4):
        for held in (keys_a, keys_b):
            held[hop] = zshift(held[hop - 1], 1)
            held[NZ - hop] = zshift(held[NZ - hop + 1], -1)
    keys_a[4] = zshift(keys_a[3], 1)
    keys_b[4] = zshift(keys_b[5], -1)

    ends = jnp.cumsum(doc_lengths[0])

    where = jnp.stack([z, y])
    keys = []
    for r in range(NZ):
        keys += [keys_a[r], keys_b[r]]
    packed, own_a, own_b, *parts = attention_grads(
        where,
        ends,
        mask_tiers[0].reshape(-1),
        keys,
        q_all,
        qg_par,
        g_all,
        extra_own,
    )
    part_a = {r: parts[2 * (r - 1)] for r in range(1, NZ)}
    part_b = {r: parts[2 * (r - 1) + 1] for r in range(1, NZ)}

    down_a = zshift(part_a[4], -1)
    up_b = zshift(part_b[4], 1)
    for r in (3, 2, 1):
        down_a = zshift(add_low(down_a, part_a[r]), -1)
        up_b = zshift(add_low(up_b, part_b[NZ - r]), 1)
    down_b = zshift(part_b[3], -1)
    up_a = zshift(part_a[5], 1)
    for r in (2, 1):
        down_b = zshift(add_low(down_b, part_b[r]), -1)
        up_a = zshift(add_low(up_a, part_a[NZ - r]), 1)

    def to_owners(rows):
        return lax.all_to_all(
            rows.reshape(2 * N_DP, CAP, -1), ("dp", "yl"), split_axis=0, concat_axis=0, tiled=True
        )

    q_rows = to_owners(packed)
    kv_packed = finish_rows(where, own_a, own_b, down_a, up_a, down_b, up_b, extra_own, qg_par)
    kv_packed, q_rows = lax.optimization_barrier((kv_packed, q_rows))
    kv_rows = to_owners(kv_packed)
    return lay_out(q_rows, kv_rows)[None, None]


def solution(mesh):
    fine = Mesh(mesh.devices.reshape(N_DP, NZ, 2), ("dp", "z", "yl"))
    rows = P("dp", ("z", "yl"), None)
    return jax.shard_map(
        per_device,
        mesh=fine,
        in_specs=(rows, rows, rows, rows, rows, P("dp", None), P("dp", None, None), rows),
        out_specs=P("dp", ("z", "yl"), None, None, None),
        check_vma=False,
    )
```

```python
import math

import jax
import jax.numpy as jnp
from jax import lax
from jax.experimental import pallas as pl
from jax.experimental.pallas import tpu as pltpu
from jax.sharding import Mesh, PartitionSpec as P

H = 32
KV = 4
HD = 128
CAP = 16
N_DP = 16
NZ = 8
ROWS = 128
BLK = 2 * ROWS
HALF_Q = H * HD // 2
HALF_KV = KV * HD // 2
HEADS_KV = H // KV
STEP_HEADS = 8
CHUNK = STEP_HEADS * HD
WIDTH = STEP_HEADS * ROWS
STEPS = 2 * HALF_Q // CHUNK
SLOTS = N_DP * 2 * CAP
LAY_OUT = 4
NEG = -1e30
F32 = jnp.float32
BF16 = jnp.bfloat16
NT = (((1,), (1,)), ((), ()))
NN = (((1,), (0,)), ((), ()))


def zshift(x, by):
    return lax.ppermute(x, "z", [(i, (i + by) % NZ) for i in range(NZ)])


def yswap(x):
    return lax.ppermute(x, "yl", [(0, 1), (1, 0)])


def zshift_yswap(x, by):
    pairs = [(2 * i + y, 2 * ((i + by) % NZ) + 1 - y) for i in range(NZ) for y in range(2)]
    return lax.ppermute(x, ("z", "yl"), pairs)


def slots_of(extra, pair_place):
    owner = extra[3 * H // 2 : 3 * H // 2 + 1].astype(jnp.int32)
    return owner * (2 * CAP) + pair_place * CAP + extra[3 * H // 2 + 1 : 3 * H // 2 + 2].astype(jnp.int32)


def grads_kernel(where_ref, ends_ref, tiers_ref, *refs):
    keys_in = refs[0:16]
    q_own, q_par, g_own, g_par, extra_own, extra_par, packed_ref = refs[16:23]
    kv_out = refs[23:39]
    (kbuf, kt, sbuf, bias, acc, dqt, onehot, mx, den, deltas, active) = refs[39:]
    step = pl.program_id(0)
    half = step // (STEPS // 2)
    z = where_ref[0]
    y = where_ref[1]
    factor = HD**-0.5
    to_log2 = factor * math.log2(math.e)

    @pl.when(step == 0)
    def _prepare():
        acc[...] = jnp.zeros_like(acc)
        for r in range(NZ):
            for part in range(2):
                start = pl.multiple_of(((z - r) & (NZ - 1)) * BLK + (y ^ part) * ROWS, ROWS)
                block = keys_in[2 * r + part][...]
                kbuf[pl.ds(start, ROWS), :] = block
                for g in range(2):
                    kt[g, :, pl.ds(start, ROWS)] = block[:, g * HD : (g + 1) * HD].T

    @pl.when(step % (STEPS // 2) == 0)
    def _mask():
        extra = jnp.where(half == 0, extra_own[...], extra_par[...]).astype(F32).T
        deltas[...] = extra[0 : H // 2] + extra[H // 2 : H] + extra[H : 3 * H // 2]
        target = slots_of(extra, y ^ half)
        base = z * BLK + ROWS * (y ^ half)
        slot = lax.broadcasted_iota(jnp.int32, (SLOTS // 2, ROWS), 0)
        slot = (slot // CAP) * (2 * CAP) + (y ^ half) * CAP + slot % CAP
        onehot[...] = jnp.where(slot == target, 1.0, 0.0).astype(BF16)
        query_pos = base + lax.broadcasted_iota(jnp.int32, (1, ROWS), 1)
        first = jnp.zeros((1, ROWS), jnp.int32)
        last = jnp.full((1, ROWS), NZ * BLK, jnp.int32)
        low = jnp.int32(0)
        high = jnp.int32(NZ * BLK)
        for d in range(8):
            end = ends_ref[d]
            first = jnp.where(end <= query_pos, jnp.maximum(first, end), first)
            last = jnp.where(end > query_pos, jnp.minimum(last, end), last)
            low = jnp.where(end <= base, jnp.maximum(low, end), low)
            high = jnp.where(end > base + ROWS - 1, jnp.minimum(high, end), high)
        last = last - 1
        i_blk = 4 * z + 2 * (y ^ half)
        low = low // ROWS
        active[0] = low
        active[1] = (high + ROWS - 1) // ROWS - low

        def mask(n, carry):
            for jb in range(2):
                j_blk = 2 * n + jb
                start = pl.multiple_of(j_blk * 64, 64)
                key_pos = start + lax.broadcasted_iota(jnp.int32, (64, ROWS), 0)
                tier = jnp.where(
                    lax.broadcasted_iota(jnp.int32, (1, ROWS), 1) < 64,
                    tiers_ref[i_blk * 32 + j_blk],
                    tiers_ref[(i_blk + 1) * 32 + j_blk],
                )
                reach = jnp.where(tier == 2, NZ * BLK, jnp.where(tier == 1, query_pos, -1))
                ok = (key_pos >= first) & (key_pos <= jnp.minimum(reach, last))
                bias[pl.ds(start, 64), :] = jnp.where(ok, 0.0, NEG)
            return carry

        lax.fori_loop(low, low + active[1], mask, 0)

    kv_head = (step // (HEADS_KV // STEP_HEADS)) % 2
    first_block = active[0]
    n_blocks = active[1]
    own = half == 0
    q_all = jnp.where(own, q_own[...], q_par[...])
    g_all = jnp.where(own, g_own[...], g_par[...])
    q = jnp.concatenate([q_all[:, h * HD : (h + 1) * HD] for h in range(STEP_HEADS)], axis=0)
    g = jnp.concatenate([g_all[:, h * HD : (h + 1) * HD] for h in range(STEP_HEADS)], axis=0)
    head = (step % (STEPS // 2)) * STEP_HEADS
    delta = jnp.concatenate([deltas[pl.ds(head + h, 1), :] for h in range(STEP_HEADS)], axis=1)
    k_cols = pl.ds(pl.multiple_of(kv_head * HD, HD), HD)
    v_cols = pl.ds(pl.multiple_of(HALF_KV + kv_head * HD, HD), HD)
    mx[...] = jnp.full_like(mx, NEG)
    den[...] = jnp.zeros_like(den)
    dqt[...] = jnp.zeros_like(dqt)

    def over_keys(body):
        def step_of(n, carry):
            body(pl.multiple_of((first_block + 4 * n) * ROWS, ROWS), 4 * ROWS)
            return carry

        lax.fori_loop(0, n_blocks // 4, step_of, 0)
        for size in (2, 1):

            @pl.when((n_blocks & size) != 0)
            def _rest(size=size):
                done = n_blocks & ~(2 * size - 1)
                body(pl.multiple_of((first_block + done) * ROWS, ROWS), size * ROWS)

    def score(start, count):
        rows = pl.ds(start, count)
        s = lax.dot_general(kbuf[rows, k_cols], q, NT, preferred_element_type=F32)
        s = s * to_log2 + jnp.concatenate([bias[rows, :]] * STEP_HEADS, axis=1)
        sbuf[rows, :] = s
        s = s.reshape(count // 8, 8, WIDTH)
        old = mx[...]
        new = jnp.maximum(old, jnp.max(s, axis=0))
        mx[...] = new
        den[...] = den[...] * jnp.exp2(old - new) + jnp.sum(jnp.exp2(s - new[None]), axis=0)

    over_keys(score)
    top = jnp.max(mx[...], axis=0, keepdims=True)
    lse = top + jnp.log2(jnp.sum(den[...] * jnp.exp2(mx[...] - top), axis=0, keepdims=True))

    def backward(start, count):
        rows = pl.ds(start, count)
        w = jnp.exp2(sbuf[rows, :] - lse)
        dp = lax.dot_general(kbuf[rows, v_cols], g, NT, preferred_element_type=F32)
        ds = (w * (dp - delta)).astype(BF16)
        acc[rows, v_cols] += lax.dot_general(w.astype(BF16), g, NN, preferred_element_type=F32)
        acc[rows, k_cols] += lax.dot_general(ds, q, NN, preferred_element_type=F32)
        dqt[...] += lax.dot_general(kt[kv_head, :, rows], ds, NN, preferred_element_type=F32)

    over_keys(backward)
    low_dq = (dqt[...] * factor).astype(BF16)
    for h in range(STEP_HEADS):
        packed_ref[:, 0, :, h * HD : (h + 1) * HD] = (
            lax.dot_general(onehot[...], low_dq[:, h * ROWS : (h + 1) * ROWS], NT, preferred_element_type=F32)
            .astype(BF16)
            .reshape(N_DP, CAP, HD)
        )

    @pl.when(step == STEPS - 1)
    def _finish():
        for r in range(NZ):
            for part in range(2):
                out = kv_out[2 * r + part]
                rows = pl.ds(pl.multiple_of(((z - r) & (NZ - 1)) * BLK + (y ^ part) * ROWS, ROWS), ROWS)
                out[:, :HALF_KV] = (acc[rows, :HALF_KV] * factor).astype(out.dtype)
                out[:, HALF_KV:] = acc[rows, HALF_KV:].astype(out.dtype)


def attention_grads(where, ends, tiers, keys, q_all, qg_par, g_all, extra_own):
    block = pl.BlockSpec((ROWS, 2 * HALF_KV), lambda c, where, ends, tiers: (0, 0))
    extra = pl.BlockSpec((ROWS, HD), lambda c, where, ends, tiers: (0, 0))
    extra_par = pl.BlockSpec((ROWS, HD), lambda c, where, ends, tiers: (0, 2 * HALF_Q // HD))
    per_half = STEPS // 2

    def own_at(c, where, ends, tiers):
        return 0, where[1] * per_half + jnp.minimum(c, per_half - 1)

    def partner_at(c, where, ends, tiers):
        return 0, jnp.maximum(c - per_half, 0)

    def partner_g_at(c, where, ends, tiers):
        return 0, per_half + jnp.maximum(c - per_half, 0)

    def out_at(c, where, ends, tiers):
        return 0, where[1] ^ (c // per_half), 0, c % per_half

    own = pl.BlockSpec((ROWS, CHUNK), own_at)
    partner = pl.BlockSpec((ROWS, CHUNK), partner_at)
    partner_g = pl.BlockSpec((ROWS, CHUNK), partner_g_at)
    kv_bf16 = jax.ShapeDtypeStruct((ROWS, 2 * HALF_KV), BF16)
    kv_f32 = jax.ShapeDtypeStruct((ROWS, 2 * HALF_KV), F32)
    return pl.pallas_call(
        grads_kernel,
        grid_spec=pltpu.PrefetchScalarGridSpec(
            num_scalar_prefetch=3,
            grid=(STEPS,),
            in_specs=[block] * 16 + [own, partner, own, partner_g, extra, extra_par],
            out_specs=[pl.BlockSpec((N_DP, 1, CAP, CHUNK), out_at)] + [block] * 16,
            scratch_shapes=[
                pltpu.VMEM((NZ * BLK, 2 * HALF_KV), BF16),
                pltpu.VMEM((2, HD, NZ * BLK), BF16),
                pltpu.VMEM((NZ * BLK, WIDTH), F32),
                pltpu.VMEM((NZ * BLK, ROWS), F32),
                pltpu.VMEM((NZ * BLK, 2 * HALF_KV), F32),
                pltpu.VMEM((HD, WIDTH), F32),
                pltpu.VMEM((SLOTS // 2, ROWS), BF16),
                pltpu.VMEM((8, WIDTH), F32),
                pltpu.VMEM((8, WIDTH), F32),
                pltpu.VMEM((H // 2, ROWS), F32),
                pltpu.SMEM((2,), jnp.int32),
            ],
        ),
        out_shape=[jax.ShapeDtypeStruct((N_DP, 2, CAP, HALF_Q), BF16)] + [kv_f32] * 2 + [kv_bf16] * 14,
        compiler_params=pltpu.CompilerParams(
            dimension_semantics=("arbitrary",), vmem_limit_bytes=56 * 1024 * 1024
        ),
        cost_estimate=pl.CostEstimate(flops=8 * 10**9, bytes_accessed=10 * 2**20, transcendentals=4 * 10**6),
        name="grads",
    )(where, ends, tiers, *keys, q_all, qg_par, g_all, qg_par, extra_own, qg_par)


def finish_kernel(where_ref, own_a, own_b, down_a, up_a, down_b, up_b, extra_own, extra_par, out):
    y = where_ref[1]
    target = jnp.concatenate(
        [slots_of(extra_own[...].astype(F32).T, y), slots_of(extra_par[...].astype(F32).T, 1 - y)], axis=1
    )
    slot = lax.broadcasted_iota(jnp.int32, (SLOTS, BLK), 0)
    onehot = jnp.where(slot == target, 1.0, 0.0).astype(BF16)
    a = own_a[...] + down_a[...].astype(F32) + up_a[...].astype(F32)
    b = own_b[...] + down_b[...].astype(F32) + up_b[...].astype(F32)
    rows = jnp.concatenate([a, b], axis=0).astype(BF16)
    out[...] = lax.dot_general(onehot, rows, NN, preferred_element_type=F32).astype(BF16)


def finish_rows(*operands):
    block = pl.BlockSpec((ROWS, 2 * HALF_KV), lambda c, where: (0, 0))
    extra = pl.BlockSpec((ROWS, HD), lambda c, where: (0, 0))
    extra_par = pl.BlockSpec((ROWS, HD), lambda c, where: (0, 2 * HALF_Q // HD))
    return pl.pallas_call(
        finish_kernel,
        grid_spec=pltpu.PrefetchScalarGridSpec(
            num_scalar_prefetch=1,
            grid=(1,),
            in_specs=[block] * 6 + [extra, extra_par],
            out_specs=pl.BlockSpec((SLOTS, 2 * HALF_KV), lambda c, where: (0, 0)),
        ),
        out_shape=jax.ShapeDtypeStruct((SLOTS, 2 * HALF_KV), BF16),
        compiler_params=pltpu.CompilerParams(vmem_limit_bytes=16 * 1024 * 1024),
        name="finish",
    )(*operands)


def lay_out_kernel(q_ref, kv_ref, out):
    first = pl.program_id(0) * LAY_OUT
    for n in range(LAY_OUT):
        for y in range(2):
            out[n, :, y * HALF_Q : (y + 1) * HALF_Q] = q_ref[2 * (first + n) + y]
            for part in range(2):
                start = 2 * HALF_Q + part * 2 * HALF_KV + y * HALF_KV
                out[n, :, start : start + HALF_KV] = kv_ref[2 * (first + n) + y, :, part * HALF_KV : (part + 1) * HALF_KV]


def lay_out(q_rows, kv_rows):
    width = 2 * HALF_Q + 4 * HALF_KV
    whole = pl.BlockSpec(memory_space=pltpu.VMEM)
    return pl.pallas_call(
        lay_out_kernel,
        grid=(N_DP // LAY_OUT,),
        in_specs=[whole, whole],
        out_specs=pl.BlockSpec((LAY_OUT, CAP, width), lambda n: (n, 0, 0)),
        out_shape=jax.ShapeDtypeStruct((N_DP, CAP, width), BF16),
        compiler_params=pltpu.CompilerParams(vmem_limit_bytes=16 * 1024 * 1024),
        name="lay_out",
    )(q_rows, kv_rows)


def add_low(a, b):
    return (a.astype(F32) + b.astype(F32)).astype(BF16)


def prepare_kernel(where_ref, q_half, g_all, out_all, owners_ref, send, extra_own):
    y = where_ref[0]
    lane = lax.broadcasted_iota(jnp.int32, (ROWS, HD), 1)
    row = lax.broadcasted_iota(jnp.int32, (ROWS, HD), 0)
    owners = jnp.broadcast_to(owners_ref[...].astype(F32), (ROWS, HD))
    earlier = (owners == owners.T) & (lane < row)
    slots = jnp.sum(jnp.where(earlier, 1.0, 0.0), axis=1, keepdims=True)
    head = lax.broadcasted_iota(jnp.int32, (HALF_Q, HD), 0) // HD
    pick = jnp.where(head == lax.broadcasted_iota(jnp.int32, (HALF_Q, HD), 1), 1.0, 0.0).astype(BF16)

    def extras(which):
        cols = pl.ds(pl.multiple_of(which * HALF_Q, HALF_Q), HALF_Q)
        product = g_all[:, cols].astype(F32) * out_all[:, cols].astype(F32)
        upper = product.astype(BF16)
        lower = (product - upper.astype(F32)).astype(BF16)
        delta = lax.dot_general(upper, pick, NN, preferred_element_type=F32)
        delta += lax.dot_general(lower, pick, NN, preferred_element_type=F32)
        high = delta.astype(BF16).astype(F32)
        middle = (delta - high).astype(BF16).astype(F32)
        low = delta - high - middle
        terms = high + pltpu.roll(middle, H // 2, 1) + pltpu.roll(low, H, 1)
        terms = jnp.where(lane == 3 * H // 2, owners, jnp.where(lane == 3 * H // 2 + 1, slots, terms))
        return terms.astype(BF16)

    send[:, :HALF_Q] = q_half[...]
    send[:, HALF_Q : 2 * HALF_Q] = g_all[:, pl.ds(pl.multiple_of((1 - y) * HALF_Q, HALF_Q), HALF_Q)]
    send[:, 2 * HALF_Q :] = extras(1 - y)
    extra_own[...] = extras(y)


def prepare(y, q_all, g_all, out_all, owners):
    width = 2 * HALF_Q + HD

    def whole(shape):
        return pl.BlockSpec(shape, lambda n, where: (0, 0))

    return pl.pallas_call(
        prepare_kernel,
        grid_spec=pltpu.PrefetchScalarGridSpec(
            num_scalar_prefetch=1,
            grid=(1,),
            in_specs=[
                pl.BlockSpec((ROWS, HALF_Q), lambda n, where: (0, 1 - where[0])),
                whole((ROWS, 2 * HALF_Q)),
                whole((ROWS, 2 * HALF_Q)),
                whole((ROWS, 1)),
            ],
            out_specs=[whole((ROWS, width)), whole((ROWS, HD))],
        ),
        out_shape=[jax.ShapeDtypeStruct((ROWS, width), BF16), jax.ShapeDtypeStruct((ROWS, HD), BF16)],
        compiler_params=pltpu.CompilerParams(vmem_limit_bytes=56 * 1024 * 1024),
        name="prepare",
    )(y[None], q_all, g_all, out_all, owners)


def per_device(queries, key_rows, value_rows, forward_out, out_grads, doc_lengths, mask_tiers, row_owners):
    z = lax.axis_index("z").astype(jnp.int32)
    y = lax.axis_index("yl").astype(jnp.int32)
    q_all, g_all = queries[0], out_grads[0]

    def half(x, which, width):
        return lax.dynamic_slice_in_dim(x, which * width, width, 1)

    def key_values(which):
        return jnp.concatenate(
            [half(key_rows[0], which, HALF_KV), half(value_rows[0], which, HALF_KV)], axis=1
        )

    a = key_values(y)
    b = key_values(1 - y)
    keys_a = {0: a, 1: zshift(a, 1), 7: zshift(a, -1)}
    keys_b = {0: yswap(b)}
    send, extra_own = prepare(y, q_all, g_all, forward_out[0], row_owners[0])
    send, keys_b[0] = lax.optimization_barrier((send, keys_b[0]))
    qg_par = yswap(send)
    for hop in range(1, 4):
        for held in (keys_a, keys_b):
            if hop not in held:
                held[hop] = zshift(held[hop - 1], 1)
                held[NZ - hop] = zshift(held[(NZ - hop + 1) % NZ], -1)
    keys_a[4] = zshift(keys_a[3], 1)
    keys_b[4] = zshift(keys_b[5], -1)

    ends = jnp.cumsum(doc_lengths[0])

    where = jnp.stack([z, y])
    keys = []
    for r in range(NZ):
        keys += [keys_a[r], keys_b[r]]
    packed, own_a, own_b, *parts = attention_grads(
        where,
        ends,
        mask_tiers[0].reshape(-1),
        keys,
        q_all,
        qg_par,
        g_all,
        extra_own,
    )
    part_a = {r: parts[2 * (r - 1)] for r in range(1, NZ)}
    part_b = {r: parts[2 * (r - 1) + 1] for r in range(1, NZ)}

    down_a = zshift(part_a[4], -1)
    up_b = zshift(part_b[4], 1)
    for r in (3, 2, 1):
        down_a = zshift(add_low(down_a, part_a[r]), -1)
        up_b = zshift(add_low(up_b, part_b[NZ - r]), 1)
    down_b = zshift(part_b[3], -1)
    up_a = zshift(part_a[5], 1)
    for r in (2, 1):
        down_b = zshift(add_low(down_b, part_b[r]), -1)
        up_a = zshift(add_low(up_a, part_a[NZ - r]), 1)

    def to_owners(rows):
        return lax.all_to_all(
            rows.reshape(2 * N_DP, CAP, -1), ("dp", "yl"), split_axis=0, concat_axis=0, tiled=True
        )

    q_rows = to_owners(packed)
    kv_packed = finish_rows(where, own_a, own_b, down_a, up_a, down_b, up_b, extra_own, qg_par)
    kv_packed, q_rows = lax.optimization_barrier((kv_packed, q_rows))
    kv_rows = to_owners(kv_packed)
    return lay_out(q_rows, kv_rows)[None, None]


def solution(mesh):
    fine = Mesh(mesh.devices.reshape(N_DP, NZ, 2), ("dp", "z", "yl"))
    rows = P("dp", ("z", "yl"), None)
    return jax.shard_map(
        per_device,
        mesh=fine,
        in_specs=(rows, rows, rows, rows, rows, P("dp", None), P("dp", None, None), rows),
        out_specs=P("dp", ("z", "yl"), None, None, None),
        check_vma=False,
    )
```

```python
import math

import jax
import jax.numpy as jnp
from jax import lax
from jax.experimental import pallas as pl
from jax.experimental.pallas import tpu as pltpu
from jax.sharding import Mesh, PartitionSpec as P

H = 32
KV = 4
HD = 128
CAP = 16
N_DP = 16
NZ = 8
ROWS = 128
BLK = 2 * ROWS
HALF_Q = H * HD // 2
HALF_KV = KV * HD // 2
HEADS = H // KV
WIDTH = HEADS * ROWS
CHUNK = HALF_Q
SLOTS = N_DP * 2 * CAP
LAY_OUT = 4
NEG = -1e30
F32 = jnp.float32
BF16 = jnp.bfloat16
NT = (((1,), (1,)), ((), ()))
NN = (((1,), (0,)), ((), ()))


def zshift(x, by):
    return lax.ppermute(x, "z", [(i, (i + by) % NZ) for i in range(NZ)])


def yswap(x):
    return lax.ppermute(x, "yl", [(0, 1), (1, 0)])


def zshift_yswap(x, by):
    pairs = [(2 * i + y, 2 * ((i + by) % NZ) + 1 - y) for i in range(NZ) for y in range(2)]
    return lax.ppermute(x, ("z", "yl"), pairs)


def slots_of(extra, pair_place):
    owner = extra[3 * H // 2 : 3 * H // 2 + 1].astype(jnp.int32)
    return owner * (2 * CAP) + pair_place * CAP + extra[3 * H // 2 + 1 : 3 * H // 2 + 2].astype(jnp.int32)


def grads_kernel(where_ref, ends_ref, tiers_ref, *refs):
    keys_in = refs[0:16]
    q_own, q_par, g_own, g_par, extra_own, extra_par, packed_ref = refs[16:23]
    kv_out = refs[23:39]
    (kbuf, kt, sbuf, bias, acc, dqt, onehot, mx, den, deltas) = refs[39:]
    step = pl.program_id(0)
    half = step
    z = where_ref[0]
    y = where_ref[1]
    factor = HD**-0.5
    to_log2 = factor * math.log2(math.e)

    @pl.when(step == 0)
    def _prepare():
        acc[...] = jnp.zeros_like(acc)
        for r in range(NZ):
            for part in range(2):
                start = pl.multiple_of(((z - r) & (NZ - 1)) * BLK + (y ^ part) * ROWS, ROWS)
                block = keys_in[2 * r + part][...]
                kbuf[pl.ds(start, ROWS), :] = block
                for g in range(2):
                    kt[g, :, pl.ds(start, ROWS)] = block[:, g * HD : (g + 1) * HD].T

    extra = jnp.where(half == 0, extra_own[...], extra_par[...]).astype(F32).T
    deltas[...] = extra[0 : H // 2] + extra[H // 2 : H] + extra[H : 3 * H // 2]
    target = slots_of(extra, y ^ half)
    base = z * BLK + ROWS * (y ^ half)
    slot = lax.broadcasted_iota(jnp.int32, (SLOTS // 2, ROWS), 0)
    slot = (slot // CAP) * (2 * CAP) + (y ^ half) * CAP + slot % CAP
    onehot[...] = jnp.where(slot == target, 1.0, 0.0).astype(BF16)
    query_pos = base + lax.broadcasted_iota(jnp.int32, (1, ROWS), 1)
    first = jnp.zeros((1, ROWS), jnp.int32)
    last = jnp.full((1, ROWS), NZ * BLK, jnp.int32)
    low = jnp.int32(0)
    high = jnp.int32(NZ * BLK)
    for d in range(8):
        end = ends_ref[d]
        first = jnp.where(end <= query_pos, jnp.maximum(first, end), first)
        last = jnp.where(end > query_pos, jnp.minimum(last, end), last)
        low = jnp.where(end <= base, jnp.maximum(low, end), low)
        high = jnp.where(end > base + ROWS - 1, jnp.minimum(high, end), high)
    last = last - 1
    i_blk = 4 * z + 2 * (y ^ half)
    low = low // ROWS
    first_block = low
    n_blocks = (high + ROWS - 1) // ROWS - low

    def mask(n, carry):
        for jb in range(2):
            j_blk = 2 * n + jb
            start = pl.multiple_of(j_blk * 64, 64)
            key_pos = start + lax.broadcasted_iota(jnp.int32, (64, ROWS), 0)
            tier = jnp.where(
                lax.broadcasted_iota(jnp.int32, (1, ROWS), 1) < 64,
                tiers_ref[i_blk * 32 + j_blk],
                tiers_ref[(i_blk + 1) * 32 + j_blk],
            )
            reach = jnp.where(tier == 2, NZ * BLK, jnp.where(tier == 1, query_pos, -1))
            ok = (key_pos >= first) & (key_pos <= jnp.minimum(reach, last))
            bias[pl.ds(start, 64), :] = jnp.where(ok, 0.0, NEG)
        return carry

    lax.fori_loop(low, low + n_blocks, mask, 0)

    own = half == 0
    q_all = jnp.where(own, q_own[...], q_par[...])
    g_all = jnp.where(own, g_own[...], g_par[...])
    groups = []
    for kv_head in range(2):
        heads = range(kv_head * HEADS, (kv_head + 1) * HEADS)
        groups.append(
            (
                slice(kv_head * HD, (kv_head + 1) * HD),
                slice(HALF_KV + kv_head * HD, HALF_KV + (kv_head + 1) * HD),
                jnp.concatenate([q_all[:, h * HD : (h + 1) * HD] for h in heads], axis=0),
                jnp.concatenate([g_all[:, h * HD : (h + 1) * HD] for h in heads], axis=0),
                jnp.concatenate([deltas[h : h + 1, :] for h in heads], axis=1),
            )
        )
    mx[...] = jnp.full_like(mx, NEG)
    den[...] = jnp.zeros_like(den)
    dqt[...] = jnp.zeros_like(dqt)

    def over_keys(body):
        def step_of(n, carry):
            body(pl.multiple_of((first_block + 4 * n) * ROWS, ROWS), 4 * ROWS)
            return carry

        lax.fori_loop(0, n_blocks // 4, step_of, 0)
        for size in (2, 1):

            @pl.when((n_blocks & size) != 0)
            def _rest(size=size):
                done = n_blocks & ~(2 * size - 1)
                body(pl.multiple_of((first_block + done) * ROWS, ROWS), size * ROWS)

    def score(start, count):
        rows = pl.ds(start, count)
        mask = jnp.concatenate([bias[rows, :]] * HEADS, axis=1)
        for n, (k_cols, v_cols, q, g, delta) in enumerate(groups):
            s = lax.dot_general(kbuf[rows, k_cols], q, NT, preferred_element_type=F32)
            s = s * to_log2 + mask
            sbuf[n, rows, :] = s
            s = s.reshape(count // 8, 8, WIDTH)
            old = mx[n]
            new = jnp.maximum(old, jnp.max(s, axis=0))
            mx[n] = new
            den[n] = den[n] * jnp.exp2(old - new) + jnp.sum(jnp.exp2(s - new[None]), axis=0)

    over_keys(score)
    top = jnp.max(mx[...], axis=1, keepdims=True)
    lse = top + jnp.log2(jnp.sum(den[...] * jnp.exp2(mx[...] - top), axis=1, keepdims=True))

    def backward(start, count):
        rows = pl.ds(start, count)
        for n, (k_cols, v_cols, q, g, delta) in enumerate(groups):
            w = jnp.exp2(sbuf[n, rows, :] - lse[n])
            dp = lax.dot_general(kbuf[rows, v_cols], g, NT, preferred_element_type=F32)
            ds = (w * (dp - delta)).astype(BF16)
            acc[rows, v_cols] += lax.dot_general(w.astype(BF16), g, NN, preferred_element_type=F32)
            acc[rows, k_cols] += lax.dot_general(ds, q, NN, preferred_element_type=F32)
            dqt[n] += lax.dot_general(kt[n, :, rows], ds, NN, preferred_element_type=F32)

    over_keys(backward)
    low_dq = (dqt[...] * factor).astype(BF16)
    for h in range(2 * HEADS):
        rows = low_dq[h // HEADS, :, (h % HEADS) * ROWS : (h % HEADS + 1) * ROWS]
        packed_ref[:, 0, :, h * HD : (h + 1) * HD] = (
            lax.dot_general(onehot[...], rows, NT, preferred_element_type=F32).astype(BF16).reshape(N_DP, CAP, HD)
        )

    @pl.when(step == 1)
    def _finish():
        for r in range(NZ):
            for part in range(2):
                out = kv_out[2 * r + part]
                rows = pl.ds(pl.multiple_of(((z - r) & (NZ - 1)) * BLK + (y ^ part) * ROWS, ROWS), ROWS)
                out[:, :HALF_KV] = (acc[rows, :HALF_KV] * factor).astype(out.dtype)
                out[:, HALF_KV:] = acc[rows, HALF_KV:].astype(out.dtype)


def attention_grads(where, ends, tiers, keys, q_all, qg_par, g_all, extra_own):
    block = pl.BlockSpec((ROWS, 2 * HALF_KV), lambda c, where, ends, tiers: (0, 0))
    extra = pl.BlockSpec((ROWS, HD), lambda c, where, ends, tiers: (0, 0))
    extra_par = pl.BlockSpec((ROWS, HD), lambda c, where, ends, tiers: (0, 2 * HALF_Q // HD))

    def at(column):
        return pl.BlockSpec((ROWS, CHUNK), lambda c, where, ends, tiers: (0, column))

    own = pl.BlockSpec((ROWS, CHUNK), lambda c, where, ends, tiers: (0, where[1]))

    def out_at(c, where, ends, tiers):
        return 0, where[1] ^ c, 0, 0

    kv_bf16 = jax.ShapeDtypeStruct((ROWS, 2 * HALF_KV), BF16)
    kv_f32 = jax.ShapeDtypeStruct((ROWS, 2 * HALF_KV), F32)
    return pl.pallas_call(
        grads_kernel,
        grid_spec=pltpu.PrefetchScalarGridSpec(
            num_scalar_prefetch=3,
            grid=(2,),
            in_specs=[block] * 16 + [own, at(0), own, at(1), extra, extra_par],
            out_specs=[pl.BlockSpec((N_DP, 1, CAP, CHUNK), out_at)] + [block] * 16,
            scratch_shapes=[
                pltpu.VMEM((NZ * BLK, 2 * HALF_KV), BF16),
                pltpu.VMEM((2, HD, NZ * BLK), BF16),
                pltpu.VMEM((2, NZ * BLK, WIDTH), F32),
                pltpu.VMEM((NZ * BLK, ROWS), F32),
                pltpu.VMEM((NZ * BLK, 2 * HALF_KV), F32),
                pltpu.VMEM((2, HD, WIDTH), F32),
                pltpu.VMEM((SLOTS // 2, ROWS), BF16),
                pltpu.VMEM((2, 8, WIDTH), F32),
                pltpu.VMEM((2, 8, WIDTH), F32),
                pltpu.VMEM((H // 2, ROWS), F32),
            ],
        ),
        out_shape=[jax.ShapeDtypeStruct((N_DP, 2, CAP, HALF_Q), BF16)] + [kv_f32] * 2 + [kv_bf16] * 14,
        compiler_params=pltpu.CompilerParams(
            dimension_semantics=("arbitrary",), vmem_limit_bytes=56 * 1024 * 1024
        ),
        cost_estimate=pl.CostEstimate(flops=8 * 10**9, bytes_accessed=10 * 2**20, transcendentals=4 * 10**6),
        name="grads",
    )(where, ends, tiers, *keys, q_all, qg_par, g_all, qg_par, extra_own, qg_par)


def finish_kernel(where_ref, own_a, own_b, down_a, up_a, down_b, up_b, extra_own, extra_par, out):
    y = where_ref[1]
    target = jnp.concatenate(
        [slots_of(extra_own[...].astype(F32).T, y), slots_of(extra_par[...].astype(F32).T, 1 - y)], axis=1
    )
    slot = lax.broadcasted_iota(jnp.int32, (SLOTS, BLK), 0)
    onehot = jnp.where(slot == target, 1.0, 0.0).astype(BF16)
    a = own_a[...] + down_a[...].astype(F32) + up_a[...].astype(F32)
    b = own_b[...] + down_b[...].astype(F32) + up_b[...].astype(F32)
    rows = jnp.concatenate([a, b], axis=0).astype(BF16)
    out[...] = lax.dot_general(onehot, rows, NN, preferred_element_type=F32).astype(BF16)


def finish_rows(*operands):
    block = pl.BlockSpec((ROWS, 2 * HALF_KV), lambda c, where: (0, 0))
    extra = pl.BlockSpec((ROWS, HD), lambda c, where: (0, 0))
    extra_par = pl.BlockSpec((ROWS, HD), lambda c, where: (0, 2 * HALF_Q // HD))
    return pl.pallas_call(
        finish_kernel,
        grid_spec=pltpu.PrefetchScalarGridSpec(
            num_scalar_prefetch=1,
            grid=(1,),
            in_specs=[block] * 6 + [extra, extra_par],
            out_specs=pl.BlockSpec((SLOTS, 2 * HALF_KV), lambda c, where: (0, 0)),
        ),
        out_shape=jax.ShapeDtypeStruct((SLOTS, 2 * HALF_KV), BF16),
        compiler_params=pltpu.CompilerParams(vmem_limit_bytes=16 * 1024 * 1024),
        name="finish",
    )(*operands)


def lay_out_kernel(q_ref, kv_ref, out):
    first = pl.program_id(0) * LAY_OUT
    for n in range(LAY_OUT):
        for y in range(2):
            out[n, :, y * HALF_Q : (y + 1) * HALF_Q] = q_ref[2 * (first + n) + y]
            for part in range(2):
                start = 2 * HALF_Q + part * 2 * HALF_KV + y * HALF_KV
                out[n, :, start : start + HALF_KV] = kv_ref[2 * (first + n) + y, :, part * HALF_KV : (part + 1) * HALF_KV]


def lay_out(q_rows, kv_rows):
    width = 2 * HALF_Q + 4 * HALF_KV
    whole = pl.BlockSpec(memory_space=pltpu.VMEM)
    return pl.pallas_call(
        lay_out_kernel,
        grid=(N_DP // LAY_OUT,),
        in_specs=[whole, whole],
        out_specs=pl.BlockSpec((LAY_OUT, CAP, width), lambda n: (n, 0, 0)),
        out_shape=jax.ShapeDtypeStruct((N_DP, CAP, width), BF16),
        compiler_params=pltpu.CompilerParams(vmem_limit_bytes=16 * 1024 * 1024),
        name="lay_out",
    )(q_rows, kv_rows)


def add_low(a, b):
    return (a.astype(F32) + b.astype(F32)).astype(BF16)


def prepare_kernel(where_ref, q_half, g_all, out_all, owners_ref, send, extra_own):
    y = where_ref[0]
    lane = lax.broadcasted_iota(jnp.int32, (ROWS, HD), 1)
    row = lax.broadcasted_iota(jnp.int32, (ROWS, HD), 0)
    owners = jnp.broadcast_to(owners_ref[...].astype(F32), (ROWS, HD))
    earlier = (owners == owners.T) & (lane < row)
    slots = jnp.sum(jnp.where(earlier, 1.0, 0.0), axis=1, keepdims=True)
    head = lax.broadcasted_iota(jnp.int32, (HALF_Q, HD), 0) // HD
    pick = jnp.where(head == lax.broadcasted_iota(jnp.int32, (HALF_Q, HD), 1), 1.0, 0.0).astype(BF16)

    def extras(which):
        cols = pl.ds(pl.multiple_of(which * HALF_Q, HALF_Q), HALF_Q)
        product = g_all[:, cols].astype(F32) * out_all[:, cols].astype(F32)
        upper = product.astype(BF16)
        lower = (product - upper.astype(F32)).astype(BF16)
        delta = lax.dot_general(upper, pick, NN, preferred_element_type=F32)
        delta += lax.dot_general(lower, pick, NN, preferred_element_type=F32)
        high = delta.astype(BF16).astype(F32)
        middle = (delta - high).astype(BF16).astype(F32)
        low = delta - high - middle
        terms = high + pltpu.roll(middle, H // 2, 1) + pltpu.roll(low, H, 1)
        terms = jnp.where(lane == 3 * H // 2, owners, jnp.where(lane == 3 * H // 2 + 1, slots, terms))
        return terms.astype(BF16)

    send[:, :HALF_Q] = q_half[...]
    send[:, HALF_Q : 2 * HALF_Q] = g_all[:, pl.ds(pl.multiple_of((1 - y) * HALF_Q, HALF_Q), HALF_Q)]
    send[:, 2 * HALF_Q :] = extras(1 - y)
    extra_own[...] = extras(y)


def prepare(y, q_all, g_all, out_all, owners):
    width = 2 * HALF_Q + HD

    def whole(shape):
        return pl.BlockSpec(shape, lambda n, where: (0, 0))

    return pl.pallas_call(
        prepare_kernel,
        grid_spec=pltpu.PrefetchScalarGridSpec(
            num_scalar_prefetch=1,
            grid=(1,),
            in_specs=[
                pl.BlockSpec((ROWS, HALF_Q), lambda n, where: (0, 1 - where[0])),
                whole((ROWS, 2 * HALF_Q)),
                whole((ROWS, 2 * HALF_Q)),
                whole((ROWS, 1)),
            ],
            out_specs=[whole((ROWS, width)), whole((ROWS, HD))],
        ),
        out_shape=[jax.ShapeDtypeStruct((ROWS, width), BF16), jax.ShapeDtypeStruct((ROWS, HD), BF16)],
        compiler_params=pltpu.CompilerParams(vmem_limit_bytes=56 * 1024 * 1024),
        name="prepare",
    )(y[None], q_all, g_all, out_all, owners)


def per_device(queries, key_rows, value_rows, forward_out, out_grads, doc_lengths, mask_tiers, row_owners):
    z = lax.axis_index("z").astype(jnp.int32)
    y = lax.axis_index("yl").astype(jnp.int32)
    q_all, g_all = queries[0], out_grads[0]

    def half(x, which, width):
        return lax.dynamic_slice_in_dim(x, which * width, width, 1)

    def key_values(which):
        return jnp.concatenate(
            [half(key_rows[0], which, HALF_KV), half(value_rows[0], which, HALF_KV)], axis=1
        )

    a = key_values(y)
    b = key_values(1 - y)
    keys_a = {0: a, 1: zshift(a, 1), 7: zshift(a, -1)}
    keys_b = {0: yswap(b)}
    send, extra_own = prepare(y, q_all, g_all, forward_out[0], row_owners[0])
    send, keys_b[0] = lax.optimization_barrier((send, keys_b[0]))
    qg_par = yswap(send)
    for hop in range(1, 4):
        for held in (keys_a, keys_b):
            if hop not in held:
                held[hop] = zshift(held[hop - 1], 1)
                held[NZ - hop] = zshift(held[(NZ - hop + 1) % NZ], -1)
    keys_a[4] = zshift(keys_a[3], 1)
    keys_b[4] = zshift(keys_b[5], -1)

    ends = jnp.cumsum(doc_lengths[0])

    where = jnp.stack([z, y])
    keys = []
    for r in range(NZ):
        keys += [keys_a[r], keys_b[r]]
    packed, own_a, own_b, *parts = attention_grads(
        where,
        ends,
        mask_tiers[0].reshape(-1),
        keys,
        q_all,
        qg_par,
        g_all,
        extra_own,
    )
    part_a = {r: parts[2 * (r - 1)] for r in range(1, NZ)}
    part_b = {r: parts[2 * (r - 1) + 1] for r in range(1, NZ)}

    down_a = zshift(part_a[4], -1)
    up_b = zshift(part_b[4], 1)
    for r in (3, 2, 1):
        down_a = zshift(add_low(down_a, part_a[r]), -1)
        up_b = zshift(add_low(up_b, part_b[NZ - r]), 1)
    down_b = zshift(part_b[3], -1)
    up_a = zshift(part_a[5], 1)
    for r in (2, 1):
        down_b = zshift(add_low(down_b, part_b[r]), -1)
        up_a = zshift(add_low(up_a, part_a[NZ - r]), 1)

    def to_owners(rows):
        return lax.all_to_all(
            rows.reshape(2 * N_DP, CAP, -1), ("dp", "yl"), split_axis=0, concat_axis=0, tiled=True
        )

    q_rows = to_owners(packed)
    kv_packed = finish_rows(where, own_a, own_b, down_a, up_a, down_b, up_b, extra_own, qg_par)
    kv_packed, q_rows = lax.optimization_barrier((kv_packed, q_rows))
    kv_rows = to_owners(kv_packed)
    return lay_out(q_rows, kv_rows)[None, None]


def solution(mesh):
    fine = Mesh(mesh.devices.reshape(N_DP, NZ, 2), ("dp", "z", "yl"))
    rows = P("dp", ("z", "yl"), None)
    return jax.shard_map(
        per_device,
        mesh=fine,
        in_specs=(rows, rows, rows, rows, rows, P("dp", None), P("dp", None, None), rows),
        out_specs=P("dp", ("z", "yl"), None, None, None),
        check_vma=False,
    )
```

```python
import math

import jax
import jax.numpy as jnp
from jax import lax
from jax.experimental import pallas as pl
from jax.experimental.pallas import tpu as pltpu
from jax.sharding import Mesh, PartitionSpec as P

H = 32
KV = 4
HD = 128
CAP = 16
N_DP = 16
NZ = 8
ROWS = 128
BLK = 2 * ROWS
HALF_Q = H * HD // 2
HALF_KV = KV * HD // 2
HEADS = H // KV
WIDTH = HEADS * ROWS
CHUNK = HALF_Q
SLOTS = N_DP * 2 * CAP
LAY_OUT = 2
NEG = -1e30
F32 = jnp.float32
BF16 = jnp.bfloat16
NT = (((1,), (1,)), ((), ()))
NN = (((1,), (0,)), ((), ()))


def zshift(x, by):
    return lax.ppermute(x, "z", [(i, (i + by) % NZ) for i in range(NZ)])


def yswap(x):
    return lax.ppermute(x, "yl", [(0, 1), (1, 0)])


def zshift_yswap(x, by):
    pairs = [(2 * i + y, 2 * ((i + by) % NZ) + 1 - y) for i in range(NZ) for y in range(2)]
    return lax.ppermute(x, ("z", "yl"), pairs)


def slots_of(extra, pair_place):
    owner = extra[3 * H // 2 : 3 * H // 2 + 1].astype(jnp.int32)
    return owner * (2 * CAP) + pair_place * CAP + extra[3 * H // 2 + 1 : 3 * H // 2 + 2].astype(jnp.int32)


def grads_kernel(where_ref, ends_ref, tiers_ref, *refs):
    keys_in = refs[0:16]
    q_own, q_par, g_own, g_par, extra_own, extra_par, packed_ref = refs[16:23]
    kv_out = refs[23:39]
    (kbuf, kt, sbuf, bias, acc, dqt, onehot, mx, den, deltas) = refs[39:]
    step = pl.program_id(0)
    half = step
    z = where_ref[0]
    y = where_ref[1]
    factor = HD**-0.5
    to_log2 = factor * math.log2(math.e)

    @pl.when(step == 0)
    def _prepare():
        acc[...] = jnp.zeros_like(acc)
        for r in range(NZ):
            for part in range(2):
                start = pl.multiple_of(((z - r) & (NZ - 1)) * BLK + (y ^ part) * ROWS, ROWS)
                block = keys_in[2 * r + part][...]
                kbuf[pl.ds(start, ROWS), :] = block
                for g in range(2):
                    kt[g, :, pl.ds(start, ROWS)] = block[:, g * HD : (g + 1) * HD].T

    extra = jnp.where(half == 0, extra_own[...], extra_par[...]).astype(F32).T
    deltas[...] = extra[0 : H // 2] + extra[H // 2 : H] + extra[H : 3 * H // 2]
    target = slots_of(extra, y ^ half)
    base = z * BLK + ROWS * (y ^ half)
    slot = lax.broadcasted_iota(jnp.int32, (SLOTS // 2, ROWS), 0)
    slot = (slot // CAP) * (2 * CAP) + (y ^ half) * CAP + slot % CAP
    onehot[...] = jnp.where(slot == target, 1.0, 0.0).astype(BF16)
    query_pos = base + lax.broadcasted_iota(jnp.int32, (1, ROWS), 1)
    first = jnp.zeros((1, ROWS), jnp.int32)
    last = jnp.full((1, ROWS), NZ * BLK, jnp.int32)
    low = jnp.int32(0)
    high = jnp.int32(NZ * BLK)
    for d in range(8):
        end = ends_ref[d]
        first = jnp.where(end <= query_pos, jnp.maximum(first, end), first)
        last = jnp.where(end > query_pos, jnp.minimum(last, end), last)
        low = jnp.where(end <= base, jnp.maximum(low, end), low)
        high = jnp.where(end > base + ROWS - 1, jnp.minimum(high, end), high)
    last = last - 1
    i_blk = 4 * z + 2 * (y ^ half)
    low = low // ROWS
    first_block = low
    n_blocks = (high + ROWS - 1) // ROWS - low

    def mask(n, carry):
        for jb in range(2):
            j_blk = 2 * n + jb
            start = pl.multiple_of(j_blk * 64, 64)
            key_pos = start + lax.broadcasted_iota(jnp.int32, (64, ROWS), 0)
            tier = jnp.where(
                lax.broadcasted_iota(jnp.int32, (1, ROWS), 1) < 64,
                tiers_ref[i_blk * 32 + j_blk],
                tiers_ref[(i_blk + 1) * 32 + j_blk],
            )
            reach = jnp.where(tier == 2, NZ * BLK, jnp.where(tier == 1, query_pos, -1))
            ok = (key_pos >= first) & (key_pos <= jnp.minimum(reach, last))
            bias[pl.ds(start, 64), :] = jnp.where(ok, 0.0, NEG)
        return carry

    lax.fori_loop(low, low + n_blocks, mask, 0)

    own = half == 0
    q_all = jnp.where(own, q_own[...], q_par[...])
    g_all = jnp.where(own, g_own[...], g_par[...])
    groups = []
    for kv_head in range(2):
        heads = range(kv_head * HEADS, (kv_head + 1) * HEADS)
        groups.append(
            (
                slice(kv_head * HD, (kv_head + 1) * HD),
                slice(HALF_KV + kv_head * HD, HALF_KV + (kv_head + 1) * HD),
                jnp.concatenate([q_all[:, h * HD : (h + 1) * HD] for h in heads], axis=0),
                jnp.concatenate([g_all[:, h * HD : (h + 1) * HD] for h in heads], axis=0),
                jnp.concatenate([deltas[h : h + 1, :] for h in heads], axis=1),
            )
        )
    mx[...] = jnp.full_like(mx, NEG)
    den[...] = jnp.zeros_like(den)
    dqt[...] = jnp.zeros_like(dqt)

    def over_keys(body):
        def step_of(n, carry):
            body(pl.multiple_of((first_block + 4 * n) * ROWS, ROWS), 4 * ROWS)
            return carry

        lax.fori_loop(0, n_blocks // 4, step_of, 0)
        for size in (2, 1):

            @pl.when((n_blocks & size) != 0)
            def _rest(size=size):
                done = n_blocks & ~(2 * size - 1)
                body(pl.multiple_of((first_block + done) * ROWS, ROWS), size * ROWS)

    def score(start, count):
        rows = pl.ds(start, count)
        mask = jnp.concatenate([bias[rows, :]] * HEADS, axis=1)
        for n, (k_cols, v_cols, q, g, delta) in enumerate(groups):
            s = lax.dot_general(kbuf[rows, k_cols], q, NT, preferred_element_type=F32)
            s = s * to_log2 + mask
            sbuf[n, rows, :] = s
            s = s.reshape(count // 8, 8, WIDTH)
            old = mx[n]
            new = jnp.maximum(old, jnp.max(s, axis=0))
            mx[n] = new
            den[n] = den[n] * jnp.exp2(old - new) + jnp.sum(jnp.exp2(s - new[None]), axis=0)

    over_keys(score)
    top = jnp.max(mx[...], axis=1, keepdims=True)
    lse = top + jnp.log2(jnp.sum(den[...] * jnp.exp2(mx[...] - top), axis=1, keepdims=True))

    def backward(start, count):
        rows = pl.ds(start, count)
        for n, (k_cols, v_cols, q, g, delta) in enumerate(groups):
            w = jnp.exp2(sbuf[n, rows, :] - lse[n])
            dp = lax.dot_general(kbuf[rows, v_cols], g, NT, preferred_element_type=F32)
            ds = (w * (dp - delta)).astype(BF16)
            acc[rows, v_cols] += lax.dot_general(w.astype(BF16), g, NN, preferred_element_type=F32)
            acc[rows, k_cols] += lax.dot_general(ds, q, NN, preferred_element_type=F32)
            dqt[n] += lax.dot_general(kt[n, :, rows], ds, NN, preferred_element_type=F32)

    over_keys(backward)
    low_dq = (dqt[...] * factor).astype(BF16)
    for h in range(2 * HEADS):
        rows = low_dq[h // HEADS, :, (h % HEADS) * ROWS : (h % HEADS + 1) * ROWS]
        packed_ref[:, 0, :, h * HD : (h + 1) * HD] = (
            lax.dot_general(onehot[...], rows, NT, preferred_element_type=F32).astype(BF16).reshape(N_DP, CAP, HD)
        )

    @pl.when(step == 1)
    def _finish():
        for r in range(NZ):
            for part in range(2):
                out = kv_out[2 * r + part]
                rows = pl.ds(pl.multiple_of(((z - r) & (NZ - 1)) * BLK + (y ^ part) * ROWS, ROWS), ROWS)
                out[:, :HALF_KV] = (acc[rows, :HALF_KV] * factor).astype(out.dtype)
                out[:, HALF_KV:] = acc[rows, HALF_KV:].astype(out.dtype)


def attention_grads(where, ends, tiers, keys, q_all, qg_par, g_all, extra_own):
    block = pl.BlockSpec((ROWS, 2 * HALF_KV), lambda c, where, ends, tiers: (0, 0))
    extra = pl.BlockSpec((ROWS, HD), lambda c, where, ends, tiers: (0, 0))
    whole = pl.BlockSpec(memory_space=pltpu.VMEM)
    extra_par = pl.BlockSpec((ROWS, HD), lambda c, where, ends, tiers: (0, 2 * HALF_Q // HD))

    def at(column):
        return pl.BlockSpec((ROWS, CHUNK), lambda c, where, ends, tiers: (0, column))

    own = pl.BlockSpec((ROWS, CHUNK), lambda c, where, ends, tiers: (0, where[1]))

    def out_at(c, where, ends, tiers):
        return 0, where[1] ^ c, 0, 0

    kv_bf16 = jax.ShapeDtypeStruct((ROWS, 2 * HALF_KV), BF16)
    kv_f32 = jax.ShapeDtypeStruct((ROWS, 2 * HALF_KV), F32)
    return pl.pallas_call(
        grads_kernel,
        grid_spec=pltpu.PrefetchScalarGridSpec(
            num_scalar_prefetch=3,
            grid=(2,),
            in_specs=[whole] * 16 + [own, at(0), own, at(1), extra, extra_par],
            out_specs=[pl.BlockSpec((N_DP, 1, CAP, CHUNK), out_at)] + [whole] * 16,
            scratch_shapes=[
                pltpu.VMEM((NZ * BLK, 2 * HALF_KV), BF16),
                pltpu.VMEM((2, HD, NZ * BLK), BF16),
                pltpu.VMEM((2, NZ * BLK, WIDTH), F32),
                pltpu.VMEM((NZ * BLK, ROWS), F32),
                pltpu.VMEM((NZ * BLK, 2 * HALF_KV), F32),
                pltpu.VMEM((2, HD, WIDTH), F32),
                pltpu.VMEM((SLOTS // 2, ROWS), BF16),
                pltpu.VMEM((2, 8, WIDTH), F32),
                pltpu.VMEM((2, 8, WIDTH), F32),
                pltpu.VMEM((H // 2, ROWS), F32),
            ],
        ),
        out_shape=[jax.ShapeDtypeStruct((N_DP, 2, CAP, HALF_Q), BF16)] + [kv_f32] * 2 + [kv_bf16] * 14,
        compiler_params=pltpu.CompilerParams(
            dimension_semantics=("arbitrary",), vmem_limit_bytes=56 * 1024 * 1024
        ),
        cost_estimate=pl.CostEstimate(flops=8 * 10**9, bytes_accessed=10 * 2**20, transcendentals=4 * 10**6),
        name="grads",
    )(where, ends, tiers, *keys, q_all, qg_par, g_all, qg_par, extra_own, qg_par)


def finish_kernel(where_ref, own_a, own_b, down_a, up_a, down_b, up_b, extra_own, extra_par, out):
    y = where_ref[1]
    target = jnp.concatenate(
        [slots_of(extra_own[...].astype(F32).T, y), slots_of(extra_par[...].astype(F32).T, 1 - y)], axis=1
    )
    slot = lax.broadcasted_iota(jnp.int32, (SLOTS, BLK), 0)
    onehot = jnp.where(slot == target, 1.0, 0.0).astype(BF16)
    a = own_a[...] + down_a[...].astype(F32) + up_a[...].astype(F32)
    b = own_b[...] + down_b[...].astype(F32) + up_b[...].astype(F32)
    rows = jnp.concatenate([a, b], axis=0).astype(BF16)
    out[...] = lax.dot_general(onehot, rows, NN, preferred_element_type=F32).astype(BF16)


def finish_rows(*operands):
    block = pl.BlockSpec((ROWS, 2 * HALF_KV), lambda c, where: (0, 0))
    extra = pl.BlockSpec((ROWS, HD), lambda c, where: (0, 0))
    extra_par = pl.BlockSpec((ROWS, HD), lambda c, where: (0, 2 * HALF_Q // HD))
    return pl.pallas_call(
        finish_kernel,
        grid_spec=pltpu.PrefetchScalarGridSpec(
            num_scalar_prefetch=1,
            grid=(1,),
            in_specs=[block] * 6 + [extra, extra_par],
            out_specs=pl.BlockSpec((SLOTS, 2 * HALF_KV), lambda c, where: (0, 0)),
        ),
        out_shape=jax.ShapeDtypeStruct((SLOTS, 2 * HALF_KV), BF16),
        compiler_params=pltpu.CompilerParams(vmem_limit_bytes=16 * 1024 * 1024),
        name="finish",
    )(*operands)


def lay_out_kernel(q_ref, kv_ref, out):
    first = pl.program_id(0) * LAY_OUT
    for n in range(LAY_OUT):
        for y in range(2):
            out[n, :, y * HALF_Q : (y + 1) * HALF_Q] = q_ref[2 * (first + n) + y]
            for part in range(2):
                start = 2 * HALF_Q + part * 2 * HALF_KV + y * HALF_KV
                out[n, :, start : start + HALF_KV] = kv_ref[2 * (first + n) + y, :, part * HALF_KV : (part + 1) * HALF_KV]


def lay_out(q_rows, kv_rows):
    width = 2 * HALF_Q + 4 * HALF_KV
    whole = pl.BlockSpec(memory_space=pltpu.VMEM)
    return pl.pallas_call(
        lay_out_kernel,
        grid=(N_DP // LAY_OUT,),
        in_specs=[whole, whole],
        out_specs=pl.BlockSpec((LAY_OUT, CAP, width), lambda n: (n, 0, 0)),
        out_shape=jax.ShapeDtypeStruct((N_DP, CAP, width), BF16),
        compiler_params=pltpu.CompilerParams(vmem_limit_bytes=16 * 1024 * 1024),
        name="lay_out",
    )(q_rows, kv_rows)


def add_low(a, b):
    return (a.astype(F32) + b.astype(F32)).astype(BF16)


def prepare_kernel(where_ref, q_half, g_all, out_all, owners_ref, send, extra_own):
    y = where_ref[0]
    lane = lax.broadcasted_iota(jnp.int32, (ROWS, HD), 1)
    row = lax.broadcasted_iota(jnp.int32, (ROWS, HD), 0)
    others = jnp.broadcast_to(owners_ref[...].astype(F32), (ROWS, HD))
    owners = others.T
    earlier = (owners == others) & (lane < row)
    slots = jnp.sum(jnp.where(earlier, 1.0, 0.0), axis=1, keepdims=True)
    head = lax.broadcasted_iota(jnp.int32, (HALF_Q, HD), 0) // HD
    pick = jnp.where(head == lax.broadcasted_iota(jnp.int32, (HALF_Q, HD), 1), 1.0, 0.0).astype(BF16)

    def extras(which):
        cols = pl.ds(pl.multiple_of(which * HALF_Q, HALF_Q), HALF_Q)
        product = g_all[:, cols].astype(F32) * out_all[:, cols].astype(F32)
        upper = product.astype(BF16)
        lower = (product - upper.astype(F32)).astype(BF16)
        delta = lax.dot_general(upper, pick, NN, preferred_element_type=F32)
        delta += lax.dot_general(lower, pick, NN, preferred_element_type=F32)
        high = delta.astype(BF16).astype(F32)
        middle = (delta - high).astype(BF16).astype(F32)
        low = delta - high - middle
        terms = high + pltpu.roll(middle, H // 2, 1) + pltpu.roll(low, H, 1)
        terms = jnp.where(lane == 3 * H // 2, owners, jnp.where(lane == 3 * H // 2 + 1, slots, terms))
        return terms.astype(BF16)

    send[:, :HALF_Q] = q_half[...]
    send[:, HALF_Q : 2 * HALF_Q] = g_all[:, pl.ds(pl.multiple_of((1 - y) * HALF_Q, HALF_Q), HALF_Q)]
    send[:, 2 * HALF_Q :] = extras(1 - y)
    extra_own[...] = extras(y)


def prepare(y, q_all, g_all, out_all, owners):
    width = 2 * HALF_Q + HD

    def whole(shape):
        return pl.BlockSpec(shape, lambda n, where: (0, 0))

    return pl.pallas_call(
        prepare_kernel,
        grid_spec=pltpu.PrefetchScalarGridSpec(
            num_scalar_prefetch=1,
            grid=(1,),
            in_specs=[
                pl.BlockSpec((ROWS, HALF_Q), lambda n, where: (0, 1 - where[0])),
                whole((ROWS, 2 * HALF_Q)),
                whole((ROWS, 2 * HALF_Q)),
                whole((1, ROWS)),
            ],
            out_specs=[whole((ROWS, width)), whole((ROWS, HD))],
        ),
        out_shape=[jax.ShapeDtypeStruct((ROWS, width), BF16), jax.ShapeDtypeStruct((ROWS, HD), BF16)],
        compiler_params=pltpu.CompilerParams(vmem_limit_bytes=56 * 1024 * 1024),
        name="prepare",
    )(y[None], q_all, g_all, out_all, owners)


def per_device(queries, key_rows, value_rows, forward_out, out_grads, doc_lengths, mask_tiers, row_owners):
    z = lax.axis_index("z").astype(jnp.int32)
    y = lax.axis_index("yl").astype(jnp.int32)
    q_all, g_all = queries[0], out_grads[0]

    def half(x, which, width):
        return lax.dynamic_slice_in_dim(x, which * width, width, 1)

    def key_values(which):
        return jnp.concatenate(
            [half(key_rows[0], which, HALF_KV), half(value_rows[0], which, HALF_KV)], axis=1
        )

    a = key_values(y)
    b = key_values(1 - y)
    keys_a = {0: a, 1: zshift(a, 1), 7: zshift(a, -1)}
    keys_b = {0: yswap(b)}
    send, extra_own = prepare(y, q_all, g_all, forward_out[0], row_owners[0].reshape(1, ROWS))
    send, keys_b[0] = lax.optimization_barrier((send, keys_b[0]))
    qg_par = yswap(send)
    for hop in range(1, 4):
        for held in (keys_a, keys_b):
            if hop not in held:
                held[hop] = zshift(held[hop - 1], 1)
                held[NZ - hop] = zshift(held[(NZ - hop + 1) % NZ], -1)
    keys_a[4] = zshift(keys_a[3], 1)
    keys_b[4] = zshift(keys_b[5], -1)

    ends = jnp.cumsum(doc_lengths[0])

    where = jnp.stack([z, y])
    keys = []
    for r in range(NZ):
        keys += [keys_a[r], keys_b[r]]
    packed, own_a, own_b, *parts = attention_grads(
        where,
        ends,
        mask_tiers[0].reshape(-1),
        keys,
        q_all,
        qg_par,
        g_all,
        extra_own,
    )
    part_a = {r: parts[2 * (r - 1)] for r in range(1, NZ)}
    part_b = {r: parts[2 * (r - 1) + 1] for r in range(1, NZ)}

    down_a = zshift(part_a[4], -1)
    up_b = zshift(part_b[4], 1)
    for r in (3, 2, 1):
        down_a = zshift(add_low(down_a, part_a[r]), -1)
        up_b = zshift(add_low(up_b, part_b[NZ - r]), 1)
    down_b = zshift(part_b[3], -1)
    up_a = zshift(part_a[5], 1)
    for r in (2, 1):
        down_b = zshift(add_low(down_b, part_b[r]), -1)
        up_a = zshift(add_low(up_a, part_a[NZ - r]), 1)

    def to_owners(rows):
        return lax.all_to_all(
            rows.reshape(2 * N_DP, CAP, -1), ("dp", "yl"), split_axis=0, concat_axis=0, tiled=True
        )

    q_rows = to_owners(packed)
    kv_packed = finish_rows(where, own_a, own_b, down_a, up_a, down_b, up_b, extra_own, qg_par)
    kv_packed, q_rows = lax.optimization_barrier((kv_packed, q_rows))
    kv_rows = to_owners(kv_packed)
    return lay_out(q_rows, kv_rows)[None, None]


def solution(mesh):
    fine = Mesh(mesh.devices.reshape(N_DP, NZ, 2), ("dp", "z", "yl"))
    rows = P("dp", ("z", "yl"), None)
    return jax.shard_map(
        per_device,
        mesh=fine,
        in_specs=(rows, rows, rows, rows, rows, P("dp", None), P("dp", None, None), rows),
        out_specs=P("dp", ("z", "yl"), None, None, None),
        check_vma=False,
    )
```
